128 devices in a mesh: pool: 4 (over z_lo, core), dev: 32 (over x, y, z_hi).
Axes of the slice: x: 4, y: 4, z: 4 (z_hi: 2, z_lo: 2; z = z_hi * 2 + z_lo), core: 2. Of those that a mesh axis runs over, the one named last changes fastest.
Arguments:
- hidden_in: bfloat16 [32, 7168], P('pool', 'dev'), may hold values from -32 to 32
- in_gain: float32 [7168], P('dev'), may hold values from 0.25 to 1.75
- w_latent: bfloat16 [7168, 2560], P('dev'), may hold values from -0.0625 to 0.0625
- q_gain: float32 [2048], replicated, may hold values from 0.25 to 1.75
- w_query: bfloat16 [2048, 16384], P(None, 'dev'), may hold values from -0.125 to 0.125
- cache_keys: bfloat16 [32, 16384, 256], P('pool', 'dev'), may hold values from -240 to 240
- cache_values: bfloat16 [32, 16384, 256], P('pool', 'dev'), may hold values from -6 to 6
- lengths: int32 [32], P('pool'), may hold values from 1 to 16384, 262144 in all
- w_out: bfloat16 [16384, 7168], P('dev'), may hold values from -0.1875 to 0.1875
- post_gain: float32 [7168], P('dev'), may hold values from 0.25 to 1.75
- w_gate: bfloat16 [7168, 18432], P(None, ('pool', 'dev')), may hold values from -0.0625 to 0.0625
- w_up: bfloat16 [7168, 18432], P(None, ('pool', 'dev')), may hold values from -0.0625 to 0.0625
- w_down: bfloat16 [18432, 7168], P(('pool', 'dev')), may hold values from -0.15625 to 0.15625
Outputs:
- mixed: float32 [32, 7168], P('pool', 'dev')
The draws below stay inside these ranges and needn't reach their ends.
All inputs are finite; a program needn't handle non-finite values. No bound on the sum of `lengths` on one device may be relied on, other than what follows from the above.
Results may differ from the reference program's by a relative error of at most 0.013.
Values may be sent and summed in bfloat16 or wider, within the bound.
A program may use at most 128 MiB of HBM per device.

```python
import math
import jax
import jax.numpy as jnp
import numpy as np
from jax import lax

D = 7168
H = 64
HD = 256
QR = 2048
FF = 18432
ROWS = 32
CACHE = 16384


def draw_hidden_in(key, part):
    key = jax.random.fold_in(key, 1)
    row_key, col_key, field_key = jax.random.split(key, 3)
    row_scale = jnp.exp(jax.random.uniform(row_key, (ROWS, 1), jnp.float32, math.log(0.4), math.log(2.5)))
    col_spread = jnp.exp(jax.random.uniform(col_key, (1, D), jnp.float32, math.log(0.75), math.log(1.33)))
    ramp = jnp.arange(D, dtype=jnp.float32)[None, :] / (D - 1)
    col_scale = jnp.exp(math.log(0.5) + math.log(10.0) * ramp) * col_spread
    base_field = jnp.clip(jax.random.normal(field_key, (ROWS, D), jnp.float32), -4.0, 4.0)
    return jnp.clip(base_field * row_scale * col_scale, -32.0, 32.0).astype(jnp.bfloat16)


def draw_cache_keys(key, part):
    key = jax.random.fold_in(key, 2)
    base_field = jnp.clip(jax.random.normal(key, (ROWS, CACHE, HD), jnp.float32), -4.0, 4.0)
    return base_field.astype(jnp.bfloat16)


def strengthened(drawn, key, source, target, parts, factor):
    def block_of(position):
        return (jnp.arange(drawn.shape[position]) // (drawn.shape[position] // parts)).reshape((-1,) + (1,) * (drawn.ndim - 1 - position))

    near = jax.random.permutation(key, parts)[block_of(target)]
    second = (block_of(target) + parts // 2) % parts
    return jnp.where((block_of(source) == near) | (block_of(source) == second), factor * drawn, drawn)


def block_scale(rng, dims, cuts, least, largest):
    def one(dim, blocks):
        heights = jax.random.uniform(jax.random.fold_in(jax.random.fold_in(rng, 6), dim), (blocks,), jnp.float32, least / len(cuts), largest / len(cuts))
        return jnp.repeat(jnp.exp(heights), dims[dim] // blocks).reshape((-1,) + (1,) * (len(dims) - dim - 1))

    factor_of = one(*cuts[0])
    for cut in cuts[1:]:
        factor_of = factor_of * one(*cut)
    return factor_of


def split_up(count, total, limit, skew):
    loads = [(1 << 20) // math.isqrt(rank ** skew) + 1 for rank in range(2, count + 1)]
    surplus, given = total - limit - (count - 1), [1] * (count - 1)
    while surplus > 0:
        free = [i for i in range(count - 1) if given[i] < limit]
        whole, budget = sum([loads[i] for i in free]), surplus
        for i in free:
            extra = min(limit - given[i], max(1, budget * loads[i] // whole), surplus)
            given[i] = given[i] + extra
            surplus = surplus - extra
    return np.array([limit] + given)


def ragged(key, number_of, total, reach, slope):
    if number_of == 2:
        one = jax.random.randint(key, (), max(1, total - reach), min(reach, total - 1) + 1)
        return jnp.stack([one, total - one])
    sizes = jnp.asarray(split_up(number_of, total, reach, slope), jnp.int32)
    pairs = (number_of - 1) // 2
    giver, taker = sizes[1:1 + 2 * pairs:2], sizes[2:2 + 2 * pairs:2]
    margin = jnp.minimum(giver - 1, reach - taker)
    passed = jax.random.randint(jax.random.fold_in(key, 1), (pairs,), 0, 1 << 20) % (margin + 1)
    sizes = sizes.at[1:1 + 2 * pairs:2].set(giver - passed).at[2:2 + 2 * pairs:2].set(taker + passed)
    return sizes[jax.random.permutation(jax.random.fold_in(key, 2), number_of)]


def noise(own_key, extent, spread, reach, shards=(), held_as=jnp.bfloat16):
    entries = jax.random.normal(own_key, extent, jnp.float32) * spread
    if len(shards) > 0:
        entries = block_scale(own_key, extent, shards, -0.22, 0.18) * entries
    return jnp.clip(entries, min=-reach, max=reach).astype(held_as)


def noise_with(stream_key, dims, scale, reach, cuts, heavy, kind=jnp.bfloat16):
    result = scale * jax.random.normal(stream_key, dims, jnp.float32)
    if cuts:
        result = result * block_scale(stream_key, dims, cuts, -0.22, 0.18)
    return jnp.clip(strengthened(result, jax.random.fold_in(stream_key, 3), *heavy), -reach, reach).astype(kind)


def setup_inputs(seed: int = 0) -> dict:
    streams_of = jax.random.split(jax.random.key(seed), 14)
    hidden_in = draw_hidden_in(jax.random.fold_in(streams_of[13], 71), 0)
    in_gain = jnp.clip(1.0 + 0.15 * jax.random.normal(streams_of[1], (D,), jnp.float32), 0.25, 1.75)
    w_latent = noise(streams_of[2], (D, QR + 2 * HD), D ** -0.5, 0.0625, ((0, 32),))
    q_gain = jnp.clip(1.0 + 0.15 * jax.random.normal(streams_of[3], (QR,), jnp.float32), 0.25, 1.75)
    w_query = noise(streams_of[4], (QR, H * HD), QR ** -0.5, 0.125, ((1, 32),))
    cache_keys = draw_cache_keys(jax.random.fold_in(streams_of[13], 71), 0)
    cache_values = noise(streams_of[6], (ROWS, CACHE, HD), 1.0, 6.0, ((0, 4), (1, 32)))
    lengths = ragged(streams_of[7], ROWS, ROWS * CACHE // 2, CACHE, 2).astype(jnp.int32)
    w_out = noise_with(streams_of[8], (H * HD, D), (H * HD // 4) ** -0.5, 0.1875, ((0, 32),), (0, 1, 32, 2.75))
    post_gain = jnp.clip(1.0 + 0.15 * jax.random.normal(streams_of[9], (D,), jnp.float32), 0.25, 1.75)
    w_gate = noise(streams_of[10], (D, FF), D ** -0.5, 0.0625, ((1, 128),))
    w_up = noise(streams_of[11], (D, FF), D ** -0.5, 0.0625, ((1, 128),))
    w_down = noise_with(streams_of[12], (FF, D), FF ** -0.5, 0.15625, ((0, 128),), (0, 1, 128, 5.5))
    return dict(hidden_in=hidden_in, in_gain=in_gain, w_latent=w_latent, q_gain=q_gain, w_query=w_query, cache_keys=cache_keys, cache_values=cache_values, lengths=lengths, w_out=w_out, post_gain=post_gain, w_gate=w_gate, w_up=w_up, w_down=w_down)


EPS = 1e-05
NEG = -1e+30

def attend_block(items):
    query, keys, values, key_new, value_new, length = items
    scale_inv = 1.0 / math.sqrt(HD)
    query_f = query.astype(jnp.float32)
    scores = jnp.einsum('bhd,bpd->bhp', query_f, keys.astype(jnp.float32)) * scale_inv
    fresh = lax.optimization_barrier(jnp.sum(query_f * key_new.astype(jnp.float32)[:, None, :], axis=-1)) * scale_inv
    positions = jnp.arange(CACHE, dtype=jnp.int32)
    valid_mask = (positions[None, :] < length[:, None])[:, None, :]
    masked = jnp.where(valid_mask, scores, NEG)
    highest = jnp.maximum(lax.optimization_barrier(jnp.max(masked, axis=-1)), fresh)
    weights = jnp.where(valid_mask, jnp.exp(masked - highest[..., None]), 0.0)
    fresh_weight = jnp.exp(fresh - highest)
    mass = lax.optimization_barrier(jnp.sum(weights, axis=-1)) + fresh_weight
    rounded = weights.astype(jnp.bfloat16).astype(jnp.float32)
    numerator = jnp.einsum('bhp,bpd->bhd', rounded, values.astype(jnp.float32))
    numerator = numerator + fresh_weight.astype(jnp.bfloat16).astype(jnp.float32)[..., None] * value_new.astype(jnp.float32)[:, None, :]
    return (numerator / mass[..., None]).astype(jnp.bfloat16)

def reference(hidden_in, in_gain, w_latent, q_gain, w_query, cache_keys, cache_values, lengths, w_out, post_gain, w_gate, w_up, w_down):
    hidden_f = hidden_in.astype(jnp.float32)
    row_mean = lax.optimization_barrier(jnp.mean(hidden_f * hidden_f, axis=1))
    scaled_in = (hidden_f * in_gain[None, :]).astype(jnp.bfloat16)
    latent = jnp.dot(scaled_in, w_latent, preferred_element_type=jnp.float32) * lax.rsqrt(row_mean + EPS)[:, None]
    query_latent = latent[:, :QR]
    key_new = latent[:, QR:QR + HD].astype(jnp.bfloat16)
    value_new = latent[:, QR + HD:].astype(jnp.bfloat16)
    latent_mean = lax.optimization_barrier(jnp.mean(query_latent * query_latent, axis=1))
    query_normed = (query_latent * lax.rsqrt(latent_mean + EPS)[:, None] * q_gain[None, :]).astype(jnp.bfloat16)
    query = jnp.dot(query_normed, w_query, preferred_element_type=jnp.float32).astype(jnp.bfloat16)
    blocks = ROWS // 8
    attended = lax.map(attend_block, (query.reshape(blocks, 8, H, HD), cache_keys.reshape(blocks, 8, CACHE, HD), cache_values.reshape(blocks, 8, CACHE, HD), key_new.reshape(blocks, 8, HD), value_new.reshape(blocks, 8, HD), lengths.reshape(blocks, 8)))
    attended = attended.reshape(ROWS, H * HD)
    residual = hidden_f + jnp.dot(attended, w_out, preferred_element_type=jnp.float32)
    res_mean = lax.optimization_barrier(jnp.mean(residual * residual, axis=1))
    normed = (residual * lax.rsqrt(res_mean + EPS)[:, None] * post_gain[None, :]).astype(jnp.bfloat16)
    gate_out = jnp.dot(normed, w_gate, preferred_element_type=jnp.float32)
    up_out = jnp.dot(normed, w_up, preferred_element_type=jnp.float32)
    activated = (jax.nn.silu(gate_out) * up_out).astype(jnp.bfloat16)
    return residual + jnp.dot(activated, w_down, preferred_element_type=jnp.float32)
```

```python
import math

import jax
import jax.numpy as jnp
from jax import lax
from jax.experimental import pallas as pl
from jax.experimental.pallas import tpu as pltpu
from jax.sharding import PartitionSpec as P

D = 7168
H = 64
HD = 256
QR = 2048
EPS = 1e-05
NEG = -1e30
MESH = pl.DeviceIdType.MESH

N_POOL = 4
N_DEV = 32
N_ALL = N_POOL * N_DEV
ROWS = 8
COLS = 224
LANES = 128
CHUNKS = (QR + 2 * HD) // LANES + 1
GROUP = 4
GROUP_COLS = GROUP * COLS
N_GROUP = N_DEV // GROUP
POS = 512
MSG = HD + LANES

F32 = jnp.float32
BF16 = jnp.bfloat16


def lane_of(shape):
    return lax.broadcasted_iota(jnp.int32, shape, len(shape) - 1)


def tiles_to_chunks(tiles):
    lane = lane_of(tiles[0].shape)
    t = tiles
    return (
        (t[0], t[1]),
        (jnp.where(lane < 96, t[2], t[1]), jnp.where(lane < 96, t[3], t[2])),
        (jnp.where(lane < 64, t[4], t[3]), jnp.where(lane < 64, t[5], t[4])),
        (jnp.where(lane < 32, t[6], t[5]), t[6]),
    )


def chunks_to_tiles(chunks):
    (a0, b0), (a1, b1), (a2, b2), (a3, b3) = chunks
    lane = lane_of(a0.shape)
    return (
        a0,
        jnp.where(lane < 96, b0, a1),
        jnp.where(lane < 96, a1, b1),
        jnp.where(lane < 64, b1, a2),
        jnp.where(lane < 64, a2, b2),
        jnp.where(lane < 32, b2, a3),
        jnp.where(lane < 32, a3, b3),
    )


def kernel(
    hidden_hbm, in_gain_hbm, w_latent_hbm, q_gain_hbm, w_query_hbm, keys_hbm, values_hbm, lengths_ref,
    w_out_hbm, post_gain_hbm, w_gate_hbm, w_up_hbm, w_down_hbm,
    out_ref,
    hidden_v, in_gain_v, q_gain_v, post_gain_v, w_latent, w_query, keys, values, w_out, w_gate, w_up, w_down,
    pad_hidden, pad_gain, s1, r1, s2, r2, s3, r3, q_wide, o_wide, s4, r4, s5, r5, s6, r6, x_all, s7, r7,
    local_sem, send_sem, recv_sem,
):
    p = lax.axis_index("pool")
    d = lax.axis_index("dev")

    barrier = pltpu.get_barrier_semaphore()

    def greet(k, carry):
        t = lax.rem(p * N_DEV + d + k, N_ALL)
        pl.semaphore_signal(
            barrier, inc=1, device_id=(lax.div(t, N_DEV), lax.rem(t, N_DEV)), device_id_type=MESH
        )
        return carry

    lax.fori_loop(1, N_ALL, greet, 0)

    def fetch(i, source, target):
        return pltpu.make_async_copy(source, target, local_sem.at[i])

    fetches = [
        fetch(i, source, target)
        for i, (source, target) in enumerate(
            [
                (hidden_hbm, hidden_v),
                (in_gain_hbm, in_gain_v),
                (w_latent_hbm, w_latent),
                (q_gain_hbm, q_gain_v),
                (w_query_hbm, w_query),
                (keys_hbm, keys),
                (values_hbm, values),
                (w_out_hbm, w_out),
                (post_gain_hbm, post_gain_v),
                (w_gate_hbm, w_gate),
                (w_up_hbm, w_up),
                (w_down_hbm, w_down),
            ]
        )
    ]
    for copy in fetches:
        copy.start()
    (f_hidden, f_in_gain, f_latent, f_q_gain, f_query, f_keys, f_values, f_out, f_post_gain, f_gate, f_up, f_down) = fetches

    def send(i, source, target, pool, dev):
        pltpu.make_async_remote_copy(
            src_ref=source,
            dst_ref=target,
            send_sem=send_sem.at[i],
            recv_sem=recv_sem.at[i],
            device_id=(pool, dev),
            device_id_type=MESH,
        ).start()

    def landed(sem, i, ref, count):
        block = ref.at[pl.ds(0, count)]
        pltpu.make_async_copy(block, block, sem.at[i]).wait()

    def to_group(i, source, target):
        def step(k, carry):
            send(i, source, target, p, lax.rem(d + k, N_DEV))
            return carry

        lax.fori_loop(1, N_DEV, step, 0)

    pad_hidden[...] = jnp.zeros_like(pad_hidden)
    pad_gain[...] = jnp.zeros_like(pad_gain)
    f_hidden.wait()
    f_in_gain.wait()
    hidden_f = hidden_v[...].astype(F32)
    pad_hidden[:, :COLS] = hidden_f
    square_part = jnp.sum(hidden_f * hidden_f, axis=1, keepdims=True)
    scaled_in = (hidden_f * in_gain_v[...]).astype(BF16)
    f_latent.wait()
    part = jnp.dot(scaled_in, w_latent[...], preferred_element_type=F32)
    for c in range(CHUNKS - 1):
        s1[c] = part[:, c * LANES : (c + 1) * LANES]
    s1[CHUNKS - 1] = jnp.broadcast_to(square_part, (ROWS, LANES))

    pl.semaphore_wait(barrier, N_ALL - 1)

    def send_latent(k, carry):
        c = lax.rem(d + k, CHUNKS)

        @pl.when(c != d)
        def _():
            send(0, s1.at[c], r1.at[d], p, c)

        return carry

    lax.fori_loop(0, CHUNKS, send_latent, 0)

    @pl.when(d < CHUNKS)
    def _():
        r1[d] = s1[d]
        landed(recv_sem, 0, r1, N_DEV - 1)
        total = jnp.sum(r1[...], axis=0)
        s2[...] = total
        r2[d] = total
        to_group(1, s2, r2.at[d])
        landed(recv_sem, 1, r2, CHUNKS - 1)

    @pl.when(d >= CHUNKS)
    def _():
        landed(recv_sem, 1, r2, CHUNKS)

    row_scale = lax.rsqrt(r2[CHUNKS - 1] * (1.0 / D) + EPS)
    latents = [r2[c] * row_scale for c in range(CHUNKS - 1)]
    squares = latents[0] * latents[0]
    for c in range(1, QR // LANES):
        squares = squares + latents[c] * latents[c]
    latent_mean = jnp.sum(squares, axis=1, keepdims=True) * (1.0 / QR)
    query_latent = jnp.concatenate(latents[: QR // LANES], axis=1)
    f_q_gain.wait()
    query_normed = (query_latent * lax.rsqrt(latent_mean + EPS) * q_gain_v[...]).astype(BF16)
    f_query.wait()
    query = jnp.dot(query_normed, w_query[...], preferred_element_type=F32)
    query_rows = jnp.concatenate([query[:, :HD], query[:, HD:]], axis=0).astype(BF16)
    s3[...] = query_rows
    r3[d] = query_rows
    to_group(2, s3, r3.at[d])

    def wide_new(first):
        new = jnp.concatenate(latents[first : first + HD // LANES], axis=1).astype(BF16).astype(F32)
        return jnp.concatenate([new, new], axis=0)

    key_new = wide_new(QR // LANES)
    value_new = wide_new((QR + HD) // LANES)
    scale_inv = 1.0 / math.sqrt(HD)
    score_new = jnp.sum(query_rows.astype(F32) * key_new, axis=1, keepdims=True) * scale_inv

    landed(recv_sem, 2, r3, N_DEV - 1)
    q_all = r3[...].reshape(N_DEV * 2 * ROWS, HD).astype(F32)
    q_wide[0] = q_all[:, :LANES]
    q_wide[1] = q_all[:, LANES:]
    f_keys.wait()
    f_values.wait()

    def attend(r, carry):
        own = pl.ds(r, H, stride=ROWS)
        q = jnp.concatenate([q_wide[0, own, :], q_wide[1, own, :]], axis=1).astype(BF16)
        scores = (
            lax.dot_general(q, keys[r], (((1,), (1,)), ((), ())), preferred_element_type=F32) * scale_inv
        )
        position = d * POS + lax.broadcasted_iota(jnp.int32, (H, POS), 1)
        valid = position < lengths_ref[r]
        masked = jnp.where(valid, scores, NEG)
        top = jnp.max(masked, axis=1, keepdims=True)
        weights = jnp.where(valid, jnp.exp(masked - top), 0.0)
        mass = jnp.sum(weights, axis=1, keepdims=True)
        summed = jnp.dot(weights.astype(BF16), values[r], preferred_element_type=F32)
        some = mass > 0.0
        safe = jnp.where(some, mass, 1.0)
        mean = summed / safe
        log_mass = jnp.where(some, top + jnp.log(safe), NEG)
        o_wide[0, own, :] = mean[:, :LANES]
        o_wide[1, own, :] = mean[:, LANES:]
        o_wide[2, own, :] = jnp.broadcast_to(log_mass, (H, LANES))
        return carry

    lax.fori_loop(0, ROWS, attend, 0)

    def pack(k, carry):
        j = lax.rem(d + k, N_DEV)
        rows = pl.ds(pl.multiple_of(j * 2 * ROWS, 2 * ROWS), 2 * ROWS)
        s4[j, :, :LANES] = o_wide[0, rows, :].astype(BF16)
        s4[j, :, LANES:HD] = o_wide[1, rows, :].astype(BF16)
        log_mass = o_wide[2, rows, :]
        high = log_mass.astype(BF16).astype(F32)
        rest = log_mass - high
        middle = rest.astype(BF16).astype(F32)
        low = rest - middle
        lane = lane_of(log_mass.shape)
        s4[j, :, HD:] = jnp.where(lane == 0, high, jnp.where(lane == 1, middle, low)).astype(BF16)

        @pl.when(k > 0)
        def _():
            send(3, s4.at[j], r4.at[d], p, j)

        return carry

    lax.fori_loop(0, N_DEV, pack, 0)
    r4[d] = s4[d]
    landed(recv_sem, 3, r4, N_DEV - 1)

    pieces = r4[:, :, HD:].astype(F32)
    log_all = jnp.sum(jnp.where(lane_of(pieces.shape) < 3, pieces, 0.0), axis=2, keepdims=True)
    top_all = jnp.maximum(jnp.max(log_all, axis=0), score_new)
    share = jnp.exp(log_all - top_all[None])
    fresh = jnp.exp(score_new - top_all)
    mass_all = jnp.sum(share, axis=0) + fresh
    numerator = jnp.sum(share * r4[:, :, :HD].astype(F32), axis=0)
    numerator = numerator + fresh.astype(BF16).astype(F32) * value_new
    attended = numerator / mass_all
    own_heads = jnp.concatenate([attended[:ROWS], attended[ROWS:]], axis=1).astype(BF16)

    f_out.wait()

    def project(i, carry):
        g = lax.rem(lax.div(d, GROUP) + i, N_GROUP)
        columns = pl.ds(pl.multiple_of(g * GROUP_COLS, LANES), GROUP_COLS)
        block = jnp.dot(own_heads, w_out[:, columns], preferred_element_type=F32)
        tiles = [block[:, t * LANES : (t + 1) * LANES] for t in range(GROUP_COLS // LANES)]
        for c, (low_half, high_half) in enumerate(tiles_to_chunks(tiles)):
            j = g * GROUP + c
            s5[j] = jnp.concatenate([low_half, high_half], axis=0).astype(BF16)

            @pl.when(j != d)
            def _():
                send(4, s5.at[j], r5.at[d], p, j)

        return carry

    lax.fori_loop(0, N_GROUP, project, 0)
    r5[d] = s5[d]

    turn = lax.rem(d * (COLS % LANES), LANES)
    back = lax.rem(LANES - turn, LANES)
    f_post_gain.wait()
    pad_gain[:, :COLS] = post_gain_v[...]
    lane = lane_of((ROWS, LANES))

    def unrotated(total):
        low_half = pltpu.roll(total[:ROWS], back, 1)
        high_half = pltpu.roll(total[ROWS:], back, 1)
        return low_half, jnp.where(lane < COLS - LANES, high_half, 0.0)

    landed(recv_sem, 4, r5, N_DEV - 1)
    attn_low, attn_high = unrotated(jnp.sum(r5[...].astype(F32), axis=0))
    res_low = pad_hidden[:, :LANES] + attn_low
    res_high = pad_hidden[:, LANES:] + attn_high
    row_squares = jnp.sum(res_low * res_low + res_high * res_high, axis=1, keepdims=True)
    coarse = row_squares.astype(BF16).astype(F32)
    fine = row_squares - coarse
    gained_low = res_low * pad_gain[:, :LANES]
    gained_high = res_high * pad_gain[:, LANES:]
    gained_high = jnp.where(lane == 96, coarse, jnp.where(lane == 97, fine, gained_high))
    tile = jnp.concatenate([pltpu.roll(gained_low, turn, 1), pltpu.roll(gained_high, turn, 1)], axis=0).astype(BF16)
    s6[...] = tile
    own = d * N_POOL + p
    r6[own] = tile

    def send_rows(k, carry):
        t = lax.rem(p * N_DEV + d + k, N_ALL)
        send(5, s6, r6.at[own], lax.div(t, N_DEV), lax.rem(t, N_DEV))
        return carry

    lax.fori_loop(1, N_ALL, send_rows, 0)
    landed(recv_sem, 5, r6, N_ALL - 1)

    all_rows = N_POOL * ROWS

    def assemble(g, sums):
        first = pl.multiple_of(g * GROUP * N_POOL, GROUP * N_POOL)
        block = r6[pl.ds(first, GROUP * N_POOL)].astype(F32).reshape(GROUP, N_POOL, 2, ROWS, LANES)
        chunks = [
            (block[c, :, 0].reshape(all_rows, LANES), block[c, :, 1].reshape(all_rows, LANES)) for c in range(GROUP)
        ]
        columns = pl.ds(pl.multiple_of(g * GROUP_COLS, LANES), GROUP_COLS)
        x_all[:, columns] = jnp.concatenate(chunks_to_tiles(chunks), axis=1).astype(BF16)
        return tuple(total + chunk[1] for total, chunk in zip(sums, chunks))

    zeros = jnp.zeros((all_rows, LANES), F32)
    sums = lax.fori_loop(0, N_GROUP, assemble, (zeros,) * GROUP)
    lane_all = lane_of((all_rows, LANES))
    kept = zeros
    for c in range(GROUP):
        at = (96 + c * (COLS % LANES)) % LANES
        kept = kept + jnp.where((lane_all == at) | (lane_all == at + 1), sums[c], 0.0)
    all_squares = jnp.sum(kept, axis=1, keepdims=True)
    norm = lax.rsqrt(all_squares * (1.0 / D) + EPS)

    f_gate.wait()
    f_up.wait()
    transposed = (((1,), (1,)), ((), ()))
    gate = lax.dot_general(x_all[...], w_gate[...], transposed, preferred_element_type=F32) * norm
    up = lax.dot_general(x_all[...], w_up[...], transposed, preferred_element_type=F32) * norm
    activated = (gate / (1.0 + jnp.exp(-gate)) * up).astype(BF16)

    f_down.wait()

    def give(i, carry):
        g = lax.rem(lax.div(d, GROUP) + i, N_GROUP)
        columns = pl.ds(pl.multiple_of(g * GROUP_COLS, LANES), GROUP_COLS)
        block = jnp.dot(activated, w_down[:, columns], preferred_element_type=F32)
        tiles = [block[:, t * LANES : (t + 1) * LANES] for t in range(GROUP_COLS // LANES)]
        for c, (low_half, high_half) in enumerate(tiles_to_chunks(tiles)):
            j = g * GROUP + c
            for q in range(N_POOL):
                rows = slice(q * ROWS, (q + 1) * ROWS)
                at = j * N_POOL + q
                s7[at] = jnp.concatenate([low_half[rows], high_half[rows]], axis=0).astype(BF16)

                @pl.when(at != own)
                def _():
                    send(6, s7.at[at], r7.at[own], q, j)

        return carry

    lax.fori_loop(0, N_GROUP, give, 0)
    r7[own] = s7[own]
    landed(recv_sem, 6, r7, N_ALL - 1)
    ffn_low, ffn_high = unrotated(jnp.sum(r7[...].astype(F32), axis=0))
    out_ref[:, :LANES] = res_low + ffn_low
    out_ref[:, LANES:] = (res_high + ffn_high)[:, : COLS - LANES]

    @pl.when(d < CHUNKS)
    def _():
        landed(send_sem, 0, s1, CHUNKS - 1)
        landed(send_sem, 1, r1, N_DEV - 1)

    @pl.when(d >= CHUNKS)
    def _():
        landed(send_sem, 0, s1, CHUNKS)

    landed(send_sem, 2, r3, N_DEV - 1)
    landed(send_sem, 3, r4, N_DEV - 1)
    landed(send_sem, 4, r5, N_DEV - 1)
    landed(send_sem, 5, r6, N_ALL - 1)
    landed(send_sem, 6, r7, N_ALL - 1)


def local(
    hidden_in, in_gain, w_latent, q_gain, w_query, cache_keys, cache_values, lengths, w_out, post_gain,
    w_gate, w_up, w_down,
):
    operands = (
        hidden_in, in_gain[None, :], w_latent, q_gain[None, :], w_query, cache_keys, cache_values, lengths,
        w_out, post_gain[None, :], w_gate.T, w_up.T, w_down,
    )
    specs = [pl.BlockSpec(memory_space=pl.ANY)] * len(operands)
    specs[7] = pl.BlockSpec(memory_space=pltpu.SMEM)
    tile = (2 * ROWS, LANES)

    def like(array):
        return pltpu.VMEM(array.shape, array.dtype)

    scratch = [
        like(hidden_in),
        pltpu.VMEM((1, COLS), F32),
        pltpu.VMEM((1, QR), F32),
        pltpu.VMEM((1, COLS), F32),
        like(w_latent),
        like(w_query),
        like(cache_keys),
        like(cache_values),
        like(w_out),
        pltpu.VMEM(w_gate.shape[::-1], BF16),
        pltpu.VMEM(w_up.shape[::-1], BF16),
        like(w_down),
        pltpu.VMEM((ROWS, 2 * LANES), F32),
        pltpu.VMEM((1, 2 * LANES), F32),
        pltpu.VMEM((CHUNKS, ROWS, LANES), F32),
        pltpu.VMEM((N_DEV, ROWS, LANES), F32),
        pltpu.VMEM((ROWS, LANES), F32),
        pltpu.VMEM((CHUNKS, ROWS, LANES), F32),
        pltpu.VMEM((2 * ROWS, HD), BF16),
        pltpu.VMEM((N_DEV, 2 * ROWS, HD), BF16),
        pltpu.VMEM((HD // LANES, H * ROWS, LANES), F32),
        pltpu.VMEM((MSG // LANES, H * ROWS, LANES), F32),
        pltpu.VMEM((N_DEV, 2 * ROWS, MSG), BF16),
        pltpu.VMEM((N_DEV, 2 * ROWS, MSG), BF16),
        pltpu.VMEM((N_DEV, *tile), BF16),
        pltpu.VMEM((N_DEV, *tile), BF16),
        pltpu.VMEM(tile, BF16),
        pltpu.VMEM((N_ALL, *tile), BF16),
        pltpu.VMEM((N_POOL * ROWS, D), BF16),
        pltpu.VMEM((N_ALL, *tile), BF16),
        pltpu.VMEM((N_ALL, *tile), BF16),
        pltpu.SemaphoreType.DMA((12,)),
        pltpu.SemaphoreType.DMA((7,)),
        pltpu.SemaphoreType.DMA((7,)),
    ]
    return pl.pallas_call(
        kernel,
        out_shape=jax.ShapeDtypeStruct(hidden_in.shape, F32),
        in_specs=specs,
        out_specs=pl.BlockSpec(memory_space=pltpu.VMEM),
        scratch_shapes=scratch,
        compiler_params=pltpu.CompilerParams(
            collective_id=0, has_side_effects=True, vmem_limit_bytes=56 * 2**20
        ),
    )(*operands)


def solution(mesh):
    placed = (
        P("pool", "dev"),
        P("dev"),
        P("dev", None),
        P(),
        P(None, "dev"),
        P("pool", "dev", None),
        P("pool", "dev", None),
        P("pool"),
        P("dev", None),
        P("dev"),
        P(None, ("pool", "dev")),
        P(None, ("pool", "dev")),
        P(("pool", "dev"), None),
    )
    return jax.shard_map(
        local, mesh=mesh, in_specs=placed, out_specs=P("pool", "dev"), check_vma=False
    )
```

```python
import math

import jax
import jax.numpy as jnp
from jax import lax
from jax.experimental import pallas as pl
from jax.experimental.pallas import tpu as pltpu
from jax.sharding import PartitionSpec as P

D = 7168
H = 64
HD = 256
QR = 2048
EPS = 1e-05
NEG = -1e30
MESH = pl.DeviceIdType.MESH

N_POOL = 4
N_DEV = 32
N_HALF = 2 * N_DEV
ROWS = 8
COLS = 224
LANES = 128
CHUNKS = (QR + 2 * HD) // LANES + 1
GROUP = 4
GROUP_COLS = GROUP * COLS
N_GROUP = N_DEV // GROUP
POS = 512
MSG = HD + LANES
UNROLL = 8

F32 = jnp.float32
BF16 = jnp.bfloat16


def lane_of(shape):
    return lax.broadcasted_iota(jnp.int32, shape, len(shape) - 1)


def tiles_to_chunks(tiles):
    lane = lane_of(tiles[0].shape)
    t = tiles
    return (
        (t[0], t[1]),
        (jnp.where(lane < 96, t[2], t[1]), jnp.where(lane < 96, t[3], t[2])),
        (jnp.where(lane < 64, t[4], t[3]), jnp.where(lane < 64, t[5], t[4])),
        (jnp.where(lane < 32, t[6], t[5]), t[6]),
    )


def chunks_to_tiles(chunks):
    (a0, b0), (a1, b1), (a2, b2), (a3, b3) = chunks
    lane = lane_of(a0.shape)
    return (
        a0,
        jnp.where(lane < 96, b0, a1),
        jnp.where(lane < 96, a1, b1),
        jnp.where(lane < 64, b1, a2),
        jnp.where(lane < 64, a2, b2),
        jnp.where(lane < 32, b2, a3),
        jnp.where(lane < 32, a3, b3),
    )


def packed(values, bits):
    word = sum(value << (bits * k) for k, value in enumerate(values))
    return word - 2**32 if word >= 2**31 else word


FAR = ((2, 2), (2, 1), (1, 2), (2, 3), (3, 2), (1, 1), (3, 3), (1, 3), (3, 1), (2, 0), (0, 2), (1, 0), (0, 1), (3, 0), (0, 3), (0, 0))
FAR_X = packed([step[0] for step in FAR], 2)
FAR_Y = packed([step[1] for step in FAR], 2)
FAR_GROUP_X = packed([2, 2, 1, 3, 1, 3, 0, 0], 2)
FAR_GROUP_Y = packed([1, 0, 1, 1, 0, 0, 1, 0], 2)
PLANE = 16
EXTRA = CHUNKS - PLANE


def entry(word, k):
    return lax.bitwise_and(lax.shift_right_logical(jnp.int32(word), 2 * k), 3)


def kernel(
    hidden_hbm, in_gain_hbm, w_latent_hbm, q_gain_hbm, w_query_hbm, keys_hbm, values_hbm, lengths_hbm,
    w_out_hbm, post_gain_hbm, w_gate_hbm, w_up_hbm, w_down_hbm,
    out_ref,
    hidden_v, in_gain_v, q_gain_v, post_gain_v, lengths, w_latent, w_query, keys, values, w_out, w_gate, w_up, w_down,
    pad_hidden, pad_gain, s1, r1, s2, r2, s3, r3, q_wide, o_wide, s4, r4, s5, r5, s6, r6, x_all, kept, t7, u7, s7, r7,
    local_sem, send_sem, recv_sem, pair_sem,
):
    p = lax.axis_index("pool")
    d = lax.axis_index("dev")
    x = lax.div(d, 8)
    y = lax.rem(lax.div(d, 2), 4)
    z_high = lax.rem(d, 2)
    z_low = lax.div(p, 2)
    core = lax.rem(p, 2)
    plane = lax.div(d, 2)
    sibling = z_low * 2 + 1 - core

    def peer(i, dz):
        there = lax.rem(x + entry(FAR_X, i), 4) * 8 + lax.rem(y + entry(FAR_Y, i), 4) * 2
        return there + lax.rem(z_high + dz, 2)

    def peer_all(n):
        part = lax.rem(n, 4)
        there = peer(lax.div(n, 4), 1 - lax.div(part, 2))
        return lax.rem(z_low + lax.rem(lax.div(part + 1, 2), 2), 2) * 2 + core, there

    def fetch(i, source, target):
        copy = pltpu.make_async_copy(source, target, local_sem.at[i])
        copy.start()
        return copy

    f_hidden = fetch(0, hidden_hbm, hidden_v)
    f_in_gain = fetch(1, in_gain_hbm, in_gain_v)
    f_latent = fetch(2, w_latent_hbm, w_latent)

    barrier = pltpu.get_barrier_semaphore()

    def greet(n, carry):
        pl.semaphore_signal(barrier, inc=1, device_id=peer_all(n), device_id_type=MESH)
        return carry

    lax.fori_loop(0, N_HALF - 1, greet, 0)
    pl.semaphore_signal(barrier, inc=1, device_id=(sibling, d), device_id_type=MESH)

    f_q_gain = fetch(3, q_gain_hbm, q_gain_v)
    f_query = fetch(4, w_query_hbm, w_query)
    f_keys = fetch(5, keys_hbm, keys)
    f_lengths = fetch(6, lengths_hbm, lengths)
    f_values = fetch(7, values_hbm, values)
    f_out = fetch(8, w_out_hbm, w_out)
    f_post_gain = fetch(9, post_gain_hbm, post_gain_v)
    f_gate = fetch(10, w_gate_hbm, w_gate)
    f_up = fetch(11, w_up_hbm, w_up)
    f_down = fetch(12, w_down_hbm, w_down)

    def remote(i, source, target, pool, dev):
        return pltpu.make_async_remote_copy(
            src_ref=source,
            dst_ref=target,
            send_sem=send_sem.at[i],
            recv_sem=recv_sem.at[i],
            device_id=(pool, dev),
            device_id_type=MESH,
        )

    def send(*args):
        remote(*args).start()

    def landed(sem, i, ref, count):
        block = ref.at[pl.ds(0, count)]
        pltpu.make_async_copy(block, block, sem.at[i]).wait()

    def to_group(i, source, target):
        def step(n, carry):
            send(i, source, target, p, peer(lax.rem(n, 16), 1 - lax.div(n, 16)))
            return carry

        lax.fori_loop(0, N_DEV - 1, step, 0)

    pad_hidden[...] = jnp.zeros_like(pad_hidden)
    pad_gain[...] = jnp.zeros_like(pad_gain)
    f_hidden.wait()
    f_in_gain.wait()
    hidden_f = hidden_v[...].astype(F32)
    pad_hidden[:, :COLS] = hidden_f
    square_part = jnp.sum(hidden_f * hidden_f, axis=1, keepdims=True)
    scaled_in = (hidden_f * in_gain_v[...]).astype(BF16)
    f_latent.wait()
    part = jnp.dot(scaled_in, w_latent[...], preferred_element_type=F32)
    for c in range(CHUNKS - 1):
        s1[2 * (c % PLANE) + c // PLANE] = part[:, c * LANES : (c + 1) * LANES]
    s1[2 * (EXTRA - 1) + 1] = jnp.broadcast_to(square_part, (ROWS, LANES))

    pl.semaphore_wait(barrier, N_HALF)

    def send_latent(n, carry):
        j = peer(n, 0)
        owner = lax.div(j, 2)

        @pl.when(owner < EXTRA)
        def _():
            send(0, s1.at[pl.ds(2 * owner, 2)], r1.at[pl.ds(2 * plane, 2)], p, j)

        @pl.when(owner >= EXTRA)
        def _():
            send(0, s1.at[pl.ds(2 * owner, 1)], r1.at[pl.ds(2 * plane, 1)], p, j)

        return carry

    lax.fori_loop(0, PLANE - 1, send_latent, 0)

    def spread(tiles):
        r1[pl.ds(2 * plane, tiles)] = s1[pl.ds(2 * plane, tiles)]
        landed(recv_sem, 0, r1, (PLANE - 1) * tiles)
        for t in range(tiles):
            total = r1[t]
            for source in range(1, PLANE):
                total = total + r1[2 * source + t]
            s2[t] = total
            r2[2 * d + t] = total
        to_group(1, s2.at[pl.ds(0, tiles)], r2.at[pl.ds(2 * d, tiles)])
        landed(recv_sem, 1, r2, 2 * CHUNKS - tiles)

    @pl.when(plane < EXTRA)
    def _():
        spread(2)

    @pl.when(plane >= EXTRA)
    def _():
        spread(1)

    def summed_chunk(c):
        at = 4 * (c % PLANE) + c // PLANE
        return r2[at] + r2[at + 2]

    row_scale = lax.rsqrt(summed_chunk(CHUNKS - 1) * (1.0 / D) + EPS)
    latents = [summed_chunk(c) * row_scale for c in range(CHUNKS - 1)]
    squares = latents[0] * latents[0]
    for c in range(1, QR // LANES):
        squares = squares + latents[c] * latents[c]
    latent_mean = jnp.sum(squares, axis=1, keepdims=True) * (1.0 / QR)
    query_latent = jnp.concatenate(latents[: QR // LANES], axis=1)
    f_q_gain.wait()
    query_normed = (query_latent * lax.rsqrt(latent_mean + EPS) * q_gain_v[...]).astype(BF16)
    f_query.wait()
    query = jnp.dot(query_normed, w_query[...], preferred_element_type=F32)
    query_rows = jnp.concatenate([query[:, :HD], query[:, HD:]], axis=0).astype(BF16)
    s3[...] = query_rows
    r3[d] = query_rows
    to_group(2, s3, r3.at[d])

    def wide_new(first):
        new = jnp.concatenate(latents[first : first + HD // LANES], axis=1).astype(BF16).astype(F32)
        return jnp.concatenate([new, new], axis=0)

    key_new = wide_new(QR // LANES)
    value_new = wide_new((QR + HD) // LANES)
    scale_inv = 1.0 / math.sqrt(HD)
    score_new = jnp.sum(query_rows.astype(F32) * key_new, axis=1, keepdims=True) * scale_inv

    f_keys.wait()
    f_lengths.wait()
    f_values.wait()
    landed(recv_sem, 2, r3, N_DEV - 1)
    q_all = r3[...].reshape(N_DEV * 2 * ROWS, HD).astype(F32)
    q_wide[0] = q_all[:, :LANES]
    q_wide[1] = q_all[:, LANES:]

    def attend(r, carry):
        own = pl.ds(r, H, stride=ROWS)
        q = jnp.concatenate([q_wide[0, own, :], q_wide[1, own, :]], axis=1).astype(BF16)
        scores = (
            lax.dot_general(q, keys[r], (((1,), (1,)), ((), ())), preferred_element_type=F32) * scale_inv
        )
        position = d * POS + lax.broadcasted_iota(jnp.int32, (H, POS), 1)
        valid = position < lengths[r]
        masked = jnp.where(valid, scores, NEG)
        top = jnp.max(masked, axis=1, keepdims=True)
        weights = jnp.where(valid, jnp.exp(masked - top), 0.0)
        mass = jnp.sum(weights, axis=1, keepdims=True)
        summed = jnp.dot(weights.astype(BF16), values[r], preferred_element_type=F32)
        some = mass > 0.0
        safe = jnp.where(some, mass, 1.0)
        mean = summed / safe
        log_mass = jnp.where(some, top + jnp.log(safe), NEG)
        o_wide[0, own, :] = mean[:, :LANES]
        o_wide[1, own, :] = mean[:, LANES:]
        o_wide[2, own, :] = jnp.broadcast_to(log_mass, (H, LANES))
        return carry

    lax.fori_loop(0, ROWS, attend, 0, unroll=UNROLL)

    def pack(n, carry):
        j = peer(lax.rem(n, 16), 1 - lax.div(n, 16))
        rows = pl.ds(pl.multiple_of(j * 2 * ROWS, 2 * ROWS), 2 * ROWS)
        s4[j, :, :LANES] = o_wide[0, rows, :].astype(BF16)
        s4[j, :, LANES:HD] = o_wide[1, rows, :].astype(BF16)
        log_mass = o_wide[2, rows, :]
        high = log_mass.astype(BF16).astype(F32)
        rest = log_mass - high
        middle = rest.astype(BF16).astype(F32)
        low = rest - middle
        lane = lane_of(log_mass.shape)
        s4[j, :, HD:] = jnp.where(lane == 0, high, jnp.where(lane == 1, middle, low)).astype(BF16)

        @pl.when(n < N_DEV - 1)
        def _():
            send(3, s4.at[j], r4.at[d], p, j)

        return carry

    lax.fori_loop(0, N_DEV, pack, 0)
    r4[d] = s4[d]
    landed(recv_sem, 3, r4, N_DEV - 1)

    pieces = r4[:, :, HD:].astype(F32)
    log_all = jnp.sum(jnp.where(lane_of(pieces.shape) < 3, pieces, 0.0), axis=2, keepdims=True)
    top_all = jnp.maximum(jnp.max(log_all, axis=0), score_new)
    share = jnp.exp(log_all - top_all[None])
    fresh = jnp.exp(score_new - top_all)
    mass_all = jnp.sum(share, axis=0) + fresh
    numerator = jnp.sum(share * r4[:, :, :HD].astype(F32), axis=0)
    numerator = numerator + fresh.astype(BF16).astype(F32) * value_new
    attended = numerator / mass_all
    own_heads = jnp.concatenate([attended[:ROWS], attended[ROWS:]], axis=1).astype(BF16)

    f_out.wait()

    def group_at(i):
        return lax.rem(x + entry(FAR_GROUP_X, i), 4) * 2 + lax.rem(lax.div(y, 2) + entry(FAR_GROUP_Y, i), 2)

    def columns_of(g):
        return pl.ds(pl.multiple_of(g * GROUP_COLS, LANES), GROUP_COLS)

    def chunks_of(block):
        return tiles_to_chunks([block[:, t * LANES : (t + 1) * LANES] for t in range(GROUP_COLS // LANES)])

    def project(i, carry):
        g = group_at(i)
        block = jnp.dot(own_heads, w_out[:, columns_of(g)], preferred_element_type=F32)
        for c, halves in enumerate(chunks_of(block)):
            j = g * GROUP + c
            s5[j] = jnp.concatenate(halves, axis=0).astype(BF16)

            @pl.when(j != d)
            def _():
                send(4, s5.at[j], r5.at[d], p, j)

        return carry

    lax.fori_loop(0, N_GROUP, project, 0)
    r5[d] = s5[d]

    turn = lax.rem(d * (COLS % LANES), LANES)
    back = lax.rem(LANES - turn, LANES)
    f_post_gain.wait()
    pad_gain[:, :COLS] = post_gain_v[...]
    lane = lane_of((ROWS, LANES))

    def unrotated(total):
        low_half = pltpu.roll(total[:ROWS], back, 1)
        high_half = pltpu.roll(total[ROWS:], back, 1)
        return low_half, jnp.where(lane < COLS - LANES, high_half, 0.0)

    landed(recv_sem, 4, r5, N_DEV - 1)
    attn_low, attn_high = unrotated(jnp.sum(r5[...].astype(F32), axis=0))
    res_low = pad_hidden[:, :LANES] + attn_low
    res_high = pad_hidden[:, LANES:] + attn_high
    row_squares = jnp.sum(res_low * res_low + res_high * res_high, axis=1, keepdims=True)
    coarse = row_squares.astype(BF16).astype(F32)
    fine = row_squares - coarse
    gained_low = res_low * pad_gain[:, :LANES]
    gained_high = res_high * pad_gain[:, LANES:]
    gained_high = jnp.where(lane == 96, coarse, jnp.where(lane == 97, fine, gained_high))
    tile = jnp.concatenate([pltpu.roll(gained_low, turn, 1), pltpu.roll(gained_high, turn, 1)], axis=0).astype(BF16)
    s6[...] = tile
    own = d * 2 + z_low
    r6[core, own] = tile

    def send_rows(n, carry):
        send(5, s6, r6.at[core, own], *peer_all(n))
        return carry

    lax.fori_loop(0, N_HALF - 1, send_rows, 0)
    landed(recv_sem, 5, r6.at[0], N_HALF - 1)
    forward = remote(6, r6.at[core], r6.at[core], sibling, d)
    forward.start()
    forward.wait_recv()

    all_rows = N_POOL * ROWS

    def assemble(g, sums):
        first = pl.multiple_of(g * 2 * GROUP, 2 * GROUP)
        block = r6[:, pl.ds(first, 2 * GROUP)].astype(F32).reshape(2, GROUP, 2, 2, ROWS, LANES)
        chunks = [
            (block[:, c, :, 0].reshape(all_rows, LANES), block[:, c, :, 1].reshape(all_rows, LANES))
            for c in range(GROUP)
        ]
        x_all[:, columns_of(g)] = jnp.concatenate(chunks_to_tiles(chunks), axis=1).astype(BF16)
        return tuple(total + chunk[1] for total, chunk in zip(sums, chunks))

    zeros = jnp.zeros((all_rows, LANES), F32)
    sums = lax.fori_loop(0, N_GROUP, assemble, (zeros,) * GROUP)
    lane_all = lane_of((all_rows, LANES))
    squares_at = zeros
    for c in range(GROUP):
        at = (96 + c * (COLS % LANES)) % LANES
        squares_at = squares_at + jnp.where((lane_all == at) | (lane_all == at + 1), sums[c], 0.0)
    all_squares = jnp.sum(squares_at, axis=1, keepdims=True)
    norm = lax.rsqrt(all_squares * (1.0 / D) + EPS)

    f_gate.wait()
    f_up.wait()
    transposed = (((1,), (1,)), ((), ()))
    gate = lax.dot_general(x_all[...], w_gate[...], transposed, preferred_element_type=F32) * norm
    up = lax.dot_general(x_all[...], w_up[...], transposed, preferred_element_type=F32) * norm
    activated = (gate / (1.0 + jnp.exp(-gate)) * up).astype(BF16)

    f_down.wait()

    def give(i, carry):
        g = group_at(i)
        block = jnp.dot(activated, w_down[:, columns_of(g)], preferred_element_type=F32)
        for c, (low_half, high_half) in enumerate(chunks_of(block)):
            for q in range(N_POOL):
                rows = slice(q * ROWS, (q + 1) * ROWS)
                whole = jnp.concatenate([low_half[rows], high_half[rows]], axis=0)

                @pl.when(core == q // 2)
                def _():
                    kept[g, 2 * c + q % 2] = whole

                @pl.when(core != q // 2)
                def _():
                    t7[g, 2 * c + q % 2] = whole.astype(BF16)

        pltpu.make_async_remote_copy(
            src_ref=t7.at[g],
            dst_ref=u7.at[g],
            send_sem=send_sem.at[7],
            recv_sem=pair_sem.at[g],
            device_id=(sibling, d),
            device_id_type=MESH,
        ).start()
        return carry

    lax.fori_loop(0, N_GROUP, give, 0)

    def pass_on(i, carry):
        g = group_at(i)
        pltpu.make_async_copy(u7.at[g], u7.at[g], pair_sem.at[g]).wait()
        first = pl.multiple_of(g * 2 * GROUP, 2 * GROUP)
        s7[pl.ds(first, 2 * GROUP)] = (kept[g] + u7[g].astype(F32)).astype(BF16)
        for c in range(GROUP):
            for q in range(2):
                at = first + 2 * c + q

                @pl.when(at != own)
                def _():
                    send(8, s7.at[at], r7.at[own], q * 2 + core, g * GROUP + c)

        return carry

    lax.fori_loop(0, N_GROUP, pass_on, 0)
    r7[own] = s7[own]
    landed(recv_sem, 8, r7, N_HALF - 1)
    ffn_low, ffn_high = unrotated(jnp.sum(r7[...].astype(F32), axis=0))
    out_ref[:, :LANES] = res_low + ffn_low
    out_ref[:, LANES:] = (res_high + ffn_high)[:, : COLS - LANES]

    @pl.when(plane < EXTRA)
    def _():
        landed(send_sem, 0, s1, PLANE - 1 + EXTRA - 1)
        landed(send_sem, 1, r2, 2 * (N_DEV - 1))

    @pl.when(plane >= EXTRA)
    def _():
        landed(send_sem, 0, s1, PLANE - 1 + EXTRA)
        landed(send_sem, 1, r2, N_DEV - 1)

    landed(send_sem, 2, r3, N_DEV - 1)
    landed(send_sem, 3, r4, N_DEV - 1)
    landed(send_sem, 4, r5, N_DEV - 1)
    landed(send_sem, 5, r6.at[0], N_HALF - 1)
    forward.wait_send()
    landed(send_sem, 7, t7, N_GROUP)
    landed(send_sem, 8, r7, N_HALF - 1)


def local(
    hidden_in, in_gain, w_latent, q_gain, w_query, cache_keys, cache_values, lengths, w_out, post_gain,
    w_gate, w_up, w_down,
):
    operands = (
        hidden_in, in_gain[None, :], w_latent, q_gain[None, :], w_query, cache_keys, cache_values, lengths,
        w_out, post_gain[None, :], w_gate.T, w_up.T, w_down,
    )
    tile = (2 * ROWS, LANES)

    def like(array):
        return pltpu.VMEM(array.shape, array.dtype)

    scratch = [
        like(hidden_in),
        pltpu.VMEM((1, COLS), F32),
        pltpu.VMEM((1, QR), F32),
        pltpu.VMEM((1, COLS), F32),
        pltpu.SMEM(lengths.shape, jnp.int32),
        like(w_latent),
        like(w_query),
        like(cache_keys),
        like(cache_values),
        like(w_out),
        pltpu.VMEM(w_gate.shape[::-1], BF16),
        pltpu.VMEM(w_up.shape[::-1], BF16),
        like(w_down),
        pltpu.VMEM((ROWS, 2 * LANES), F32),
        pltpu.VMEM((1, 2 * LANES), F32),
        pltpu.VMEM((2 * PLANE, ROWS, LANES), F32),
        pltpu.VMEM((2 * PLANE, ROWS, LANES), F32),
        pltpu.VMEM((2, ROWS, LANES), F32),
        pltpu.VMEM((2 * N_DEV, ROWS, LANES), F32),
        pltpu.VMEM((2 * ROWS, HD), BF16),
        pltpu.VMEM((N_DEV, 2 * ROWS, HD), BF16),
        pltpu.VMEM((HD // LANES, H * ROWS, LANES), F32),
        pltpu.VMEM((MSG // LANES, H * ROWS, LANES), F32),
        pltpu.VMEM((N_DEV, 2 * ROWS, MSG), BF16),
        pltpu.VMEM((N_DEV, 2 * ROWS, MSG), BF16),
        pltpu.VMEM((N_DEV, *tile), BF16),
        pltpu.VMEM((N_DEV, *tile), BF16),
        pltpu.VMEM(tile, BF16),
        pltpu.VMEM((2, N_HALF, *tile), BF16),
        pltpu.VMEM((N_POOL * ROWS, D), BF16),
        pltpu.VMEM((N_GROUP, 2 * GROUP, *tile), F32),
        pltpu.VMEM((N_GROUP, 2 * GROUP, *tile), BF16),
        pltpu.VMEM((N_GROUP, 2 * GROUP, *tile), BF16),
        pltpu.VMEM((N_HALF, *tile), BF16),
        pltpu.VMEM((N_HALF, *tile), BF16),
        pltpu.SemaphoreType.DMA((13,)),
        pltpu.SemaphoreType.DMA((9,)),
        pltpu.SemaphoreType.DMA((9,)),
        pltpu.SemaphoreType.DMA((N_GROUP,)),
    ]
    return pl.pallas_call(
        kernel,
        out_shape=pltpu.VMEM(hidden_in.shape, F32),
        in_specs=[pl.BlockSpec(memory_space=pl.ANY)] * len(operands),
        out_specs=pl.BlockSpec(memory_space=pltpu.VMEM),
        scratch_shapes=scratch,
        compiler_params=pltpu.CompilerParams(
            collective_id=0, has_side_effects=True, vmem_limit_bytes=56 * 2**20
        ),
    )(*operands)


def solution(mesh):
    placed = (
        P("pool", "dev"),
        P("dev"),
        P("dev", None),
        P(),
        P(None, "dev"),
        P("pool", "dev", None),
        P("pool", "dev", None),
        P("pool"),
        P("dev", None),
        P("dev"),
        P(None, ("pool", "dev")),
        P(None, ("pool", "dev")),
        P(("pool", "dev"), None),
    )
    return jax.shard_map(
        local, mesh=mesh, in_specs=placed, out_specs=P("pool", "dev"), check_vma=False
    )
```

```python
import math

import jax
import jax.numpy as jnp
from jax import lax
from jax.experimental import pallas as pl
from jax.experimental.pallas import tpu as pltpu
from jax.sharding import PartitionSpec as P

D = 7168
H = 64
HD = 256
QR = 2048
EPS = 1e-05
NEG = -1e30
MESH = pl.DeviceIdType.MESH

N_POOL = 4
N_DEV = 32
N_HALF = 2 * N_DEV
ROWS = 8
COLS = 224
LANES = 128
CHUNKS = (QR + 2 * HD) // LANES + 1
GROUP = 4
GROUP_COLS = GROUP * COLS
N_GROUP = N_DEV // GROUP
POS = 512
MSG = HD + LANES
UNROLL = 8

F32 = jnp.float32
BF16 = jnp.bfloat16


def lane_of(shape):
    return lax.broadcasted_iota(jnp.int32, shape, len(shape) - 1)


def tiles_to_chunks(tiles):
    lane = lane_of(tiles[0].shape)
    t = tiles
    return (
        (t[0], t[1]),
        (jnp.where(lane < 96, t[2], t[1]), jnp.where(lane < 96, t[3], t[2])),
        (jnp.where(lane < 64, t[4], t[3]), jnp.where(lane < 64, t[5], t[4])),
        (jnp.where(lane < 32, t[6], t[5]), t[6]),
    )


def chunks_to_tiles(chunks):
    (a0, b0), (a1, b1), (a2, b2), (a3, b3) = chunks
    lane = lane_of(a0.shape)
    return (
        a0,
        jnp.where(lane < 96, b0, a1),
        jnp.where(lane < 96, a1, b1),
        jnp.where(lane < 64, b1, a2),
        jnp.where(lane < 64, a2, b2),
        jnp.where(lane < 32, b2, a3),
        jnp.where(lane < 32, a3, b3),
    )


def packed(values, bits):
    word = sum(value << (bits * k) for k, value in enumerate(values))
    return word - 2**32 if word >= 2**31 else word


FAR = ((2, 2), (2, 1), (1, 2), (2, 3), (3, 2), (1, 1), (3, 3), (1, 3), (3, 1), (2, 0), (0, 2), (1, 0), (0, 1), (3, 0), (0, 3), (0, 0))
FAR_X = packed([step[0] for step in FAR], 2)
FAR_Y = packed([step[1] for step in FAR], 2)
FAR_GROUP_X = packed([2, 2, 1, 3, 1, 3, 0, 0], 2)
FAR_GROUP_Y = packed([1, 0, 1, 1, 0, 0, 1, 0], 2)
PLANE = 16
EXTRA = CHUNKS - PLANE


def entry(word, k):
    return lax.bitwise_and(lax.shift_right_logical(jnp.int32(word), 2 * k), 3)


def kernel(
    hidden_hbm, in_gain_hbm, w_latent_hbm, q_gain_hbm, w_query_hbm, keys_hbm, values_hbm, lengths_hbm,
    w_out_hbm, post_gain_hbm, w_gate_hbm, w_up_hbm, w_down_hbm,
    out_ref,
    hidden_v, in_gain_v, q_gain_v, post_gain_v, lengths, w_latent, w_query, keys, values, w_out, w_gate, w_up, w_down,
    pad_hidden, pad_gain, s1, r1, s2, r2, s3, r3, q_wide, o_wide, s4, r4, s5, r5, s6, r6, x_all, s7, r7, keys_t,
    local_sem, send_sem, recv_sem,
):
    p = lax.axis_index("pool")
    d = lax.axis_index("dev")
    x = lax.div(d, 8)
    y = lax.rem(lax.div(d, 2), 4)
    z_high = lax.rem(d, 2)
    z_low = lax.div(p, 2)
    core = lax.rem(p, 2)
    plane = lax.div(d, 2)
    sibling = z_low * 2 + 1 - core

    def peer(i, dz):
        there = lax.rem(x + entry(FAR_X, i), 4) * 8 + lax.rem(y + entry(FAR_Y, i), 4) * 2
        return there + lax.rem(z_high + dz, 2)

    def peer_all(n):
        part = lax.rem(n, 4)
        there = peer(lax.div(n, 4), 1 - lax.div(part, 2))
        return lax.rem(z_low + lax.rem(lax.div(part + 1, 2), 2), 2) * 2 + core, there

    def fetch(i, source, target):
        copy = pltpu.make_async_copy(source, target, local_sem.at[i])
        copy.start()
        return copy

    f_hidden = fetch(0, hidden_hbm, hidden_v)
    f_in_gain = fetch(1, in_gain_hbm, in_gain_v)
    f_latent = fetch(2, w_latent_hbm, w_latent)

    barrier = pltpu.get_barrier_semaphore()

    def greet(n, carry):
        pl.semaphore_signal(barrier, inc=1, device_id=peer_all(n), device_id_type=MESH)
        return carry

    lax.fori_loop(0, N_HALF - 1, greet, 0)
    pl.semaphore_signal(barrier, inc=1, device_id=(sibling, d), device_id_type=MESH)

    f_q_gain = fetch(3, q_gain_hbm, q_gain_v)
    f_query = fetch(4, w_query_hbm, w_query)
    f_keys = fetch(5, keys_hbm, keys)
    f_lengths = fetch(6, lengths_hbm, lengths)
    f_values = fetch(7, values_hbm, values)
    f_out = fetch(8, w_out_hbm, w_out)
    f_post_gain = fetch(9, post_gain_hbm, post_gain_v)
    f_gate = fetch(10, w_gate_hbm, w_gate.at[0])
    f_up = fetch(11, w_up_hbm, w_up.at[0])
    f_down = fetch(12, w_down_hbm, w_down.at[0])

    def remote(i, source, target, pool, dev):
        return pltpu.make_async_remote_copy(
            src_ref=source,
            dst_ref=target,
            send_sem=send_sem.at[i],
            recv_sem=recv_sem.at[i],
            device_id=(pool, dev),
            device_id_type=MESH,
        )

    def send(*args):
        remote(*args).start()

    def landed(sem, i, ref, count):
        block = ref.at[pl.ds(0, count)]
        pltpu.make_async_copy(block, block, sem.at[i]).wait()

    def to_group(i, source, target):
        def step(n, carry):
            send(i, source, target, p, peer(lax.rem(n, 16), 1 - lax.div(n, 16)))
            return carry

        lax.fori_loop(0, N_DEV - 1, step, 0)

    pad_hidden[...] = jnp.zeros_like(pad_hidden)
    pad_gain[...] = jnp.zeros_like(pad_gain)
    f_hidden.wait()
    f_in_gain.wait()
    hidden_f = hidden_v[...].astype(F32)
    pad_hidden[:, :COLS] = hidden_f
    square_part = jnp.sum(hidden_f * hidden_f, axis=1, keepdims=True)
    scaled_in = (hidden_f * in_gain_v[...]).astype(BF16)
    f_latent.wait()
    part = jnp.dot(scaled_in, w_latent[...], preferred_element_type=F32)
    for c in range(CHUNKS - 1):
        s1[2 * (c % PLANE) + c // PLANE] = part[:, c * LANES : (c + 1) * LANES]
    s1[2 * (EXTRA - 1) + 1] = jnp.broadcast_to(square_part, (ROWS, LANES))

    pl.semaphore_wait(barrier, N_HALF)

    def send_latent(n, carry):
        j = peer(n, 0)
        owner = lax.div(j, 2)

        @pl.when(owner < EXTRA)
        def _():
            send(0, s1.at[pl.ds(2 * owner, 2)], r1.at[pl.ds(2 * plane, 2)], p, j)

        @pl.when(owner >= EXTRA)
        def _():
            send(0, s1.at[pl.ds(2 * owner, 1)], r1.at[pl.ds(2 * plane, 1)], p, j)

        return carry

    lax.fori_loop(0, PLANE - 1, send_latent, 0)

    shared = [
        remote(6 + k, source, target.at[1], sibling, d)
        for k, (source, target) in enumerate(((w_gate_hbm, w_gate), (w_up_hbm, w_up), (w_down_hbm, w_down)))
    ]
    for copy in shared:
        copy.start()

    f_keys.wait()

    def turn_keys(r, carry):
        keys_t[r] = keys[r].T
        return carry

    lax.fori_loop(0, ROWS, turn_keys, 0)

    def spread(tiles):
        r1[pl.ds(2 * plane, tiles)] = s1[pl.ds(2 * plane, tiles)]
        landed(recv_sem, 0, r1, (PLANE - 1) * tiles)
        for t in range(tiles):
            total = r1[t]
            for source in range(1, PLANE):
                total = total + r1[2 * source + t]
            s2[t] = total
            r2[2 * d + t] = total
        to_group(1, s2.at[pl.ds(0, tiles)], r2.at[pl.ds(2 * d, tiles)])
        landed(recv_sem, 1, r2, 2 * CHUNKS - tiles)

    @pl.when(plane < EXTRA)
    def _():
        spread(2)

    @pl.when(plane >= EXTRA)
    def _():
        spread(1)

    def summed_chunk(c):
        at = 4 * (c % PLANE) + c // PLANE
        return r2[at] + r2[at + 2]

    row_scale = lax.rsqrt(summed_chunk(CHUNKS - 1) * (1.0 / D) + EPS)
    latents = [summed_chunk(c) * row_scale for c in range(CHUNKS - 1)]
    squares = latents[0] * latents[0]
    for c in range(1, QR // LANES):
        squares = squares + latents[c] * latents[c]
    latent_mean = jnp.sum(squares, axis=1, keepdims=True) * (1.0 / QR)
    query_latent = jnp.concatenate(latents[: QR // LANES], axis=1)
    f_q_gain.wait()
    query_normed = (query_latent * lax.rsqrt(latent_mean + EPS) * q_gain_v[...]).astype(BF16)
    f_query.wait()
    query = jnp.dot(query_normed, w_query[...], preferred_element_type=F32)
    query_rows = jnp.concatenate([query[:, :HD], query[:, HD:]], axis=0).astype(BF16)
    s3[...] = query_rows
    r3[d] = query_rows
    to_group(2, s3, r3.at[d])

    def wide_new(first):
        new = jnp.concatenate(latents[first : first + HD // LANES], axis=1).astype(BF16).astype(F32)
        return jnp.concatenate([new, new], axis=0)

    key_new = wide_new(QR // LANES)
    value_new = wide_new((QR + HD) // LANES)
    scale_inv = 1.0 / math.sqrt(HD)
    score_new = jnp.sum(query_rows.astype(F32) * key_new, axis=1, keepdims=True) * scale_inv

    f_lengths.wait()
    f_values.wait()
    landed(recv_sem, 2, r3, N_DEV - 1)
    q_all = r3[...].reshape(N_DEV * 2 * ROWS, HD).astype(F32)
    q_wide[0] = q_all[:, :LANES]
    q_wide[1] = q_all[:, LANES:]

    def attend(r, carry):
        own = pl.ds(r, H, stride=ROWS)
        q = jnp.concatenate([q_wide[0, own, :], q_wide[1, own, :]], axis=1).astype(BF16)
        scores = jnp.dot(q, keys_t[r], preferred_element_type=F32) * scale_inv
        position = d * POS + lax.broadcasted_iota(jnp.int32, (H, POS), 1)
        valid = position < lengths[r]
        masked = jnp.where(valid, scores, NEG)
        top = jnp.max(masked, axis=1, keepdims=True)
        weights = jnp.where(valid, jnp.exp(masked - top), 0.0)
        mass = jnp.sum(weights, axis=1, keepdims=True)
        summed = jnp.dot(weights.astype(BF16), values[r], preferred_element_type=F32)
        some = mass > 0.0
        safe = jnp.where(some, mass, 1.0)
        mean = summed / safe
        log_mass = jnp.where(some, top + jnp.log(safe), NEG)
        o_wide[0, own, :] = mean[:, :LANES]
        o_wide[1, own, :] = mean[:, LANES:]
        o_wide[2, own, :] = jnp.broadcast_to(log_mass, (H, LANES))
        return carry

    lax.fori_loop(0, ROWS, attend, 0, unroll=UNROLL)

    def pack(n, carry):
        j = peer(lax.rem(n, 16), 1 - lax.div(n, 16))
        rows = pl.ds(pl.multiple_of(j * 2 * ROWS, 2 * ROWS), 2 * ROWS)
        s4[j, :, :LANES] = o_wide[0, rows, :].astype(BF16)
        s4[j, :, LANES:HD] = o_wide[1, rows, :].astype(BF16)
        log_mass = o_wide[2, rows, :]
        high = log_mass.astype(BF16).astype(F32)
        rest = log_mass - high
        middle = rest.astype(BF16).astype(F32)
        low = rest - middle
        lane = lane_of(log_mass.shape)
        s4[j, :, HD:] = jnp.where(lane == 0, high, jnp.where(lane == 1, middle, low)).astype(BF16)

        @pl.when(n < N_DEV - 1)
        def _():
            send(3, s4.at[j], r4.at[d], p, j)

        return carry

    lax.fori_loop(0, N_DEV, pack, 0)
    r4[d] = s4[d]
    landed(recv_sem, 3, r4, N_DEV - 1)

    pieces = r4[:, :, HD:].astype(F32)
    log_all = jnp.sum(jnp.where(lane_of(pieces.shape) < 3, pieces, 0.0), axis=2, keepdims=True)
    top_all = jnp.maximum(jnp.max(log_all, axis=0), score_new)
    share = jnp.exp(log_all - top_all[None])
    fresh = jnp.exp(score_new - top_all)
    mass_all = jnp.sum(share, axis=0) + fresh
    numerator = jnp.sum(share * r4[:, :, :HD].astype(F32), axis=0)
    numerator = numerator + fresh.astype(BF16).astype(F32) * value_new
    attended = numerator / mass_all
    own_heads = jnp.concatenate([attended[:ROWS], attended[ROWS:]], axis=1).astype(BF16)

    f_out.wait()

    def group_at(i):
        return lax.rem(x + entry(FAR_GROUP_X, i), 4) * 2 + lax.rem(lax.div(y, 2) + entry(FAR_GROUP_Y, i), 2)

    def columns_of(g):
        return pl.ds(pl.multiple_of(g * GROUP_COLS, LANES), GROUP_COLS)

    def chunks_of(block):
        return tiles_to_chunks([block[:, t * LANES : (t + 1) * LANES] for t in range(GROUP_COLS // LANES)])

    def project(i, carry):
        g = group_at(i)
        block = jnp.dot(own_heads, w_out[:, columns_of(g)], preferred_element_type=F32)
        for c, halves in enumerate(chunks_of(block)):
            j = g * GROUP + c
            s5[j] = jnp.concatenate(halves, axis=0).astype(BF16)

            @pl.when(j != d)
            def _():
                send(4, s5.at[j], r5.at[d], p, j)

        return carry

    lax.fori_loop(0, N_GROUP, project, 0)
    r5[d] = s5[d]

    turn = lax.rem(d * (COLS % LANES), LANES)
    back = lax.rem(LANES - turn, LANES)
    f_post_gain.wait()
    pad_gain[:, :COLS] = post_gain_v[...]
    lane = lane_of((ROWS, LANES))

    def unrotated(total):
        low_half = pltpu.roll(total[:ROWS], back, 1)
        high_half = pltpu.roll(total[ROWS:], back, 1)
        return low_half, jnp.where(lane < COLS - LANES, high_half, 0.0)

    landed(recv_sem, 4, r5, N_DEV - 1)
    attn_low, attn_high = unrotated(jnp.sum(r5[...].astype(F32), axis=0))
    res_low = pad_hidden[:, :LANES] + attn_low
    res_high = pad_hidden[:, LANES:] + attn_high
    row_squares = jnp.sum(res_low * res_low + res_high * res_high, axis=1, keepdims=True)
    coarse = row_squares.astype(BF16).astype(F32)
    fine = row_squares - coarse
    gained_low = res_low * pad_gain[:, :LANES]
    gained_high = res_high * pad_gain[:, LANES:]
    gained_high = jnp.where(lane == 96, coarse, jnp.where(lane == 97, fine, gained_high))
    tile = jnp.concatenate([pltpu.roll(gained_low, turn, 1), pltpu.roll(gained_high, turn, 1)], axis=0).astype(BF16)
    s6[...] = tile
    own = d * 2 + z_low
    r6[own] = tile

    def send_rows(n, carry):
        send(5, s6, r6.at[own], *peer_all(n))
        return carry

    lax.fori_loop(0, N_HALF - 1, send_rows, 0)
    landed(recv_sem, 5, r6, N_HALF - 1)

    some_rows = 2 * ROWS

    def assemble(g, sums):
        first = pl.multiple_of(g * 2 * GROUP, 2 * GROUP)
        block = r6[pl.ds(first, 2 * GROUP)].astype(F32).reshape(GROUP, 2, 2, ROWS, LANES)
        chunks = [
            (block[c, :, 0].reshape(some_rows, LANES), block[c, :, 1].reshape(some_rows, LANES))
            for c in range(GROUP)
        ]
        x_all[:, columns_of(g)] = jnp.concatenate(chunks_to_tiles(chunks), axis=1).astype(BF16)
        return tuple(total + chunk[1] for total, chunk in zip(sums, chunks))

    zeros = jnp.zeros((some_rows, LANES), F32)
    sums = lax.fori_loop(0, N_GROUP, assemble, (zeros,) * GROUP)
    lane_all = lane_of((some_rows, LANES))
    squares_at = zeros
    for c in range(GROUP):
        at = (96 + c * (COLS % LANES)) % LANES
        squares_at = squares_at + jnp.where((lane_all == at) | (lane_all == at + 1), sums[c], 0.0)
    all_squares = jnp.sum(squares_at, axis=1, keepdims=True)
    norm = lax.rsqrt(all_squares * (1.0 / D) + EPS)

    f_gate.wait()
    f_up.wait()
    shared[0].wait_recv()
    shared[1].wait_recv()
    transposed = (((1,), (1,)), ((), ()))

    def hidden_units(weights):
        units = weights[...].reshape(2 * weights.shape[1], D)
        return lax.dot_general(units, x_all[...], transposed, preferred_element_type=F32).T * norm

    gate = hidden_units(w_gate)
    up = hidden_units(w_up)
    activated = (gate / (1.0 + jnp.exp(-gate)) * up).astype(BF16)

    f_down.wait()
    shared[2].wait_recv()

    def pass_on(i, carry):
        g = group_at(i)
        columns = columns_of(g)
        weights = w_down[:, :, columns].reshape(2 * w_down.shape[1], GROUP_COLS)
        block = jnp.dot(activated, weights, preferred_element_type=F32)
        for c, (low_half, high_half) in enumerate(chunks_of(block)):
            for q in range(2):
                rows = slice(q * ROWS, (q + 1) * ROWS)
                at = (g * GROUP + c) * 2 + q
                s7[at] = jnp.concatenate([low_half[rows], high_half[rows]], axis=0).astype(BF16)

                @pl.when(at != own)
                def _():
                    send(9, s7.at[at], r7.at[own], q * 2 + core, g * GROUP + c)

        return carry

    lax.fori_loop(0, N_GROUP, pass_on, 0)
    r7[own] = s7[own]
    landed(recv_sem, 9, r7, N_HALF - 1)
    ffn_low, ffn_high = unrotated(jnp.sum(r7[...].astype(F32), axis=0))
    out_ref[:, :LANES] = res_low + ffn_low
    out_ref[:, LANES:] = (res_high + ffn_high)[:, : COLS - LANES]

    @pl.when(plane < EXTRA)
    def _():
        landed(send_sem, 0, s1, PLANE - 1 + EXTRA - 1)
        landed(send_sem, 1, r2, 2 * (N_DEV - 1))

    @pl.when(plane >= EXTRA)
    def _():
        landed(send_sem, 0, s1, PLANE - 1 + EXTRA)
        landed(send_sem, 1, r2, N_DEV - 1)

    landed(send_sem, 2, r3, N_DEV - 1)
    landed(send_sem, 3, r4, N_DEV - 1)
    landed(send_sem, 4, r5, N_DEV - 1)
    landed(send_sem, 5, r6, N_HALF - 1)
    for copy in shared:
        copy.wait_send()
    landed(send_sem, 9, r7, N_HALF - 1)


def local(
    hidden_in, in_gain, w_latent, q_gain, w_query, cache_keys, cache_values, lengths, w_out, post_gain,
    w_gate, w_up, w_down,
):
    operands = (
        hidden_in, in_gain[None, :], w_latent, q_gain[None, :], w_query, cache_keys, cache_values, lengths,
        w_out, post_gain[None, :], w_gate.T, w_up.T, w_down,
    )
    tile = (2 * ROWS, LANES)

    def like(array):
        return pltpu.VMEM(array.shape, array.dtype)

    scratch = [
        like(hidden_in),
        pltpu.VMEM((1, COLS), F32),
        pltpu.VMEM((1, QR), F32),
        pltpu.VMEM((1, COLS), F32),
        pltpu.SMEM(lengths.shape, jnp.int32),
        like(w_latent),
        like(w_query),
        like(cache_keys),
        like(cache_values),
        like(w_out),
        pltpu.VMEM((2, *w_gate.shape[::-1]), BF16),
        pltpu.VMEM((2, *w_up.shape[::-1]), BF16),
        pltpu.VMEM((2, *w_down.shape), BF16),
        pltpu.VMEM((ROWS, 2 * LANES), F32),
        pltpu.VMEM((1, 2 * LANES), F32),
        pltpu.VMEM((2 * PLANE, ROWS, LANES), F32),
        pltpu.VMEM((2 * PLANE, ROWS, LANES), F32),
        pltpu.VMEM((2, ROWS, LANES), F32),
        pltpu.VMEM((2 * N_DEV, ROWS, LANES), F32),
        pltpu.VMEM((2 * ROWS, HD), BF16),
        pltpu.VMEM((N_DEV, 2 * ROWS, HD), BF16),
        pltpu.VMEM((HD // LANES, H * ROWS, LANES), F32),
        pltpu.VMEM((MSG // LANES, H * ROWS, LANES), F32),
        pltpu.VMEM((N_DEV, 2 * ROWS, MSG), BF16),
        pltpu.VMEM((N_DEV, 2 * ROWS, MSG), BF16),
        pltpu.VMEM((N_DEV, *tile), BF16),
        pltpu.VMEM((N_DEV, *tile), BF16),
        pltpu.VMEM(tile, BF16),
        pltpu.VMEM((N_HALF, *tile), BF16),
        pltpu.VMEM((2 * ROWS, D), BF16),
        pltpu.VMEM((N_HALF, *tile), BF16),
        pltpu.VMEM((N_HALF, *tile), BF16),
        pltpu.VMEM((ROWS, HD, POS), BF16),
        pltpu.SemaphoreType.DMA((13,)),
        pltpu.SemaphoreType.DMA((10,)),
        pltpu.SemaphoreType.DMA((10,)),
    ]
    return pl.pallas_call(
        kernel,
        out_shape=pltpu.VMEM(hidden_in.shape, F32),
        in_specs=[pl.BlockSpec(memory_space=pl.ANY)] * len(operands),
        out_specs=pl.BlockSpec(memory_space=pltpu.VMEM),
        scratch_shapes=scratch,
        compiler_params=pltpu.CompilerParams(
            collective_id=0, has_side_effects=True, vmem_limit_bytes=56 * 2**20
        ),
    )(*operands)


def solution(mesh):
    placed = (
        P("pool", "dev"),
        P("dev"),
        P("dev", None),
        P(),
        P(None, "dev"),
        P("pool", "dev", None),
        P("pool", "dev", None),
        P("pool"),
        P("dev", None),
        P("dev"),
        P(None, ("pool", "dev")),
        P(None, ("pool", "dev")),
        P(("pool", "dev"), None),
    )
    return jax.shard_map(
        local, mesh=mesh, in_specs=placed, out_specs=P("pool", "dev"), check_vma=False
    )
```

```python
import math

import jax
import jax.numpy as jnp
from jax import lax
from jax.experimental import pallas as pl
from jax.experimental.pallas import tpu as pltpu
from jax.sharding import PartitionSpec as P

D = 7168
H = 64
HD = 256
QR = 2048
EPS = 1e-05
NEG = -1e30
MESH = pl.DeviceIdType.MESH

N_POOL = 4
N_DEV = 32
N_HALF = 2 * N_DEV
ROWS = 8
COLS = 224
LANES = 128
CHUNKS = (QR + 2 * HD) // LANES + 1
GROUP = 4
GROUP_COLS = GROUP * COLS
N_GROUP = N_DEV // GROUP
POS = 512
MSG = HD + LANES
UNROLL = 8

F32 = jnp.float32
BF16 = jnp.bfloat16


def lane_of(shape):
    return lax.broadcasted_iota(jnp.int32, shape, len(shape) - 1)


def tiles_to_chunks(tiles):
    lane = lane_of(tiles[0].shape)
    t = tiles
    return (
        (t[0], t[1]),
        (jnp.where(lane < 96, t[2], t[1]), jnp.where(lane < 96, t[3], t[2])),
        (jnp.where(lane < 64, t[4], t[3]), jnp.where(lane < 64, t[5], t[4])),
        (jnp.where(lane < 32, t[6], t[5]), t[6]),
    )


def chunks_to_tiles(chunks):
    (a0, b0), (a1, b1), (a2, b2), (a3, b3) = chunks
    lane = lane_of(a0.shape)
    return (
        a0,
        jnp.where(lane < 96, b0, a1),
        jnp.where(lane < 96, a1, b1),
        jnp.where(lane < 64, b1, a2),
        jnp.where(lane < 64, a2, b2),
        jnp.where(lane < 32, b2, a3),
        jnp.where(lane < 32, a3, b3),
    )


def packed(values, bits):
    word = sum(value << (bits * k) for k, value in enumerate(values))
    return word - 2**32 if word >= 2**31 else word


FAR = ((2, 2), (2, 1), (1, 2), (2, 3), (3, 2), (1, 1), (3, 3), (1, 3), (3, 1), (2, 0), (0, 2), (1, 0), (0, 1), (3, 0), (0, 3), (0, 0))
FAR_X = packed([step[0] for step in FAR], 2)
FAR_Y = packed([step[1] for step in FAR], 2)
FAR_GROUP_X = packed([2, 2, 1, 3, 1, 3, 0, 0], 2)
FAR_GROUP_Y = packed([1, 0, 1, 1, 0, 0, 1, 0], 2)
PLANE = 16
EXTRA = CHUNKS - PLANE


def entry(word, k):
    return lax.bitwise_and(lax.shift_right_logical(jnp.int32(word), 2 * k), 3)


def kernel(
    hidden_hbm, in_gain_hbm, w_latent_hbm, q_gain_hbm, w_query_hbm, keys_hbm, values_hbm, lengths_hbm,
    w_out_hbm, post_gain_hbm, w_gate_hbm, w_up_hbm, w_down_hbm,
    out_ref,
    hidden_v, in_gain_v, q_gain_v, post_gain_v, lengths, w_latent, w_query, keys, values, w_out, w_gate, w_up, w_down,
    pad_hidden, pad_gain, s1, r1, s2, r2, s3, r3, q_wide, o_wide, s4, r4, s5, r5, s6, r6, x_all, s7, r7, keys_t,
    local_sem, send_sem, recv_sem,
):
    p = lax.axis_index("pool")
    d = lax.axis_index("dev")
    x = lax.div(d, 8)
    y = lax.rem(lax.div(d, 2), 4)
    z_high = lax.rem(d, 2)
    z_low = lax.div(p, 2)
    core = lax.rem(p, 2)
    plane = lax.div(d, 2)
    sibling = z_low * 2 + 1 - core

    def peer(i, dz):
        there = lax.rem(x + entry(FAR_X, i), 4) * 8 + lax.rem(y + entry(FAR_Y, i), 4) * 2
        return there + lax.rem(z_high + dz, 2)

    def peer_all(n):
        part = lax.rem(n, 4)
        there = peer(lax.div(n, 4), 1 - lax.div(part, 2))
        return lax.rem(z_low + lax.rem(lax.div(part + 1, 2), 2), 2) * 2 + core, there

    def fetch(i, source, target):
        copy = pltpu.make_async_copy(source, target, local_sem.at[i])
        copy.start()
        return copy

    f_hidden = fetch(0, hidden_hbm, hidden_v)
    f_in_gain = fetch(1, in_gain_hbm, in_gain_v)
    f_latent = fetch(2, w_latent_hbm, w_latent)

    barrier = pltpu.get_barrier_semaphore()

    def greet(n, carry):
        pl.semaphore_signal(barrier, inc=1, device_id=(p, peer(n, 0)), device_id_type=MESH)
        return carry

    lax.fori_loop(0, PLANE - 1, greet, 0)
    across = 2 * (1 - z_low) + core
    other = peer(PLANE - 1, 1)
    column = ((p, other), (across, other), (across, d), (sibling, d))
    for device in column:
        pl.semaphore_signal(barrier, inc=1, device_id=device, device_id_type=MESH)

    f_q_gain = fetch(3, q_gain_hbm, q_gain_v)
    f_query = fetch(4, w_query_hbm, w_query)
    f_keys = fetch(5, keys_hbm, keys)
    f_lengths = fetch(6, lengths_hbm, lengths)
    f_values = fetch(7, values_hbm, values)
    f_out = fetch(8, w_out_hbm, w_out)
    f_post_gain = fetch(9, post_gain_hbm, post_gain_v)
    f_gate = fetch(10, w_gate_hbm, w_gate.at[0])
    f_up = fetch(11, w_up_hbm, w_up.at[0])
    f_down = fetch(12, w_down_hbm, w_down.at[0])

    def remote(i, source, target, pool, dev):
        return pltpu.make_async_remote_copy(
            src_ref=source,
            dst_ref=target,
            send_sem=send_sem.at[i],
            recv_sem=recv_sem.at[i],
            device_id=(pool, dev),
            device_id_type=MESH,
        )

    def send(*args):
        remote(*args).start()

    def landed(sem, i, ref, count):
        block = ref.at[pl.ds(0, count)]
        pltpu.make_async_copy(block, block, sem.at[i]).wait()

    def to_group(i, source, target):
        def step(n, carry):
            send(i, source, target, p, peer(lax.rem(n, 16), 1 - lax.div(n, 16)))
            return carry

        lax.fori_loop(0, N_DEV - 1, step, 0)

    pad_hidden[...] = jnp.zeros_like(pad_hidden)
    pad_gain[...] = jnp.zeros_like(pad_gain)
    f_hidden.wait()
    f_in_gain.wait()
    hidden_f = hidden_v[...].astype(F32)
    pad_hidden[:, :COLS] = hidden_f
    square_part = jnp.sum(hidden_f * hidden_f, axis=1, keepdims=True)
    scaled_in = (hidden_f * in_gain_v[...]).astype(BF16)
    f_latent.wait()
    part = jnp.dot(scaled_in, w_latent[...], preferred_element_type=F32)
    for c in range(CHUNKS - 1):
        s1[2 * (c % PLANE) + c // PLANE] = part[:, c * LANES : (c + 1) * LANES]
    s1[2 * (EXTRA - 1) + 1] = jnp.broadcast_to(square_part, (ROWS, LANES))

    pl.semaphore_wait(barrier, PLANE - 1 + len(column))

    def send_latent(n, carry):
        j = peer(n, 0)
        owner = lax.div(j, 2)

        @pl.when(owner < EXTRA)
        def _():
            send(0, s1.at[pl.ds(2 * owner, 2)], r1.at[pl.ds(2 * plane, 2)], p, j)

        @pl.when(owner >= EXTRA)
        def _():
            send(0, s1.at[pl.ds(2 * owner, 1)], r1.at[pl.ds(2 * plane, 1)], p, j)

        return carry

    lax.fori_loop(0, PLANE - 1, send_latent, 0)

    shared = [
        remote(6 + k, source, target.at[1], sibling, d)
        for k, (source, target) in enumerate(((w_gate_hbm, w_gate), (w_up_hbm, w_up), (w_down_hbm, w_down)))
    ]
    for copy in shared:
        copy.start()

    f_keys.wait()

    def turn_keys(r, carry):
        keys_t[r] = keys[r].T
        return carry

    lax.fori_loop(0, ROWS, turn_keys, 0)

    def spread(tiles):
        r1[pl.ds(2 * plane, tiles)] = s1[pl.ds(2 * plane, tiles)]
        landed(recv_sem, 0, r1, (PLANE - 1) * tiles)
        for t in range(tiles):
            total = r1[t]
            for source in range(1, PLANE):
                total = total + r1[2 * source + t]
            s2[t] = total
            r2[2 * d + t] = total
        to_group(1, s2.at[pl.ds(0, tiles)], r2.at[pl.ds(2 * d, tiles)])
        landed(recv_sem, 1, r2, 2 * CHUNKS - tiles)

    @pl.when(plane < EXTRA)
    def _():
        spread(2)

    @pl.when(plane >= EXTRA)
    def _():
        spread(1)

    def summed_chunk(c):
        at = 4 * (c % PLANE) + c // PLANE
        return r2[at] + r2[at + 2]

    row_scale = lax.rsqrt(summed_chunk(CHUNKS - 1) * (1.0 / D) + EPS)
    latents = [summed_chunk(c) * row_scale for c in range(CHUNKS - 1)]
    squares = latents[0] * latents[0]
    for c in range(1, QR // LANES):
        squares = squares + latents[c] * latents[c]
    latent_mean = jnp.sum(squares, axis=1, keepdims=True) * (1.0 / QR)
    query_latent = jnp.concatenate(latents[: QR // LANES], axis=1)
    f_q_gain.wait()
    query_normed = (query_latent * lax.rsqrt(latent_mean + EPS) * q_gain_v[...]).astype(BF16)
    f_query.wait()
    query = jnp.dot(query_normed, w_query[...], preferred_element_type=F32)
    query_rows = jnp.concatenate([query[:, :HD], query[:, HD:]], axis=0).astype(BF16)
    s3[...] = query_rows
    r3[d] = query_rows
    to_group(2, s3, r3.at[d])

    def wide_new(first):
        new = jnp.concatenate(latents[first : first + HD // LANES], axis=1).astype(BF16).astype(F32)
        return jnp.concatenate([new, new], axis=0)

    key_new = wide_new(QR // LANES)
    value_new = wide_new((QR + HD) // LANES)
    scale_inv = 1.0 / math.sqrt(HD)
    score_new = jnp.sum(query_rows.astype(F32) * key_new, axis=1, keepdims=True) * scale_inv

    f_lengths.wait()
    f_values.wait()
    landed(recv_sem, 2, r3, N_DEV - 1)
    q_all = r3[...].reshape(N_DEV * 2 * ROWS, HD).astype(F32)
    q_wide[0] = q_all[:, :LANES]
    q_wide[1] = q_all[:, LANES:]

    def attend(r, carry):
        own = pl.ds(r, H, stride=ROWS)
        q = jnp.concatenate([q_wide[0, own, :], q_wide[1, own, :]], axis=1).astype(BF16)
        scores = jnp.dot(q, keys_t[r], preferred_element_type=F32) * scale_inv
        position = d * POS + lax.broadcasted_iota(jnp.int32, (H, POS), 1)
        valid = position < lengths[r]
        masked = jnp.where(valid, scores, NEG)
        top = jnp.max(masked, axis=1, keepdims=True)
        weights = jnp.where(valid, jnp.exp(masked - top), 0.0)
        mass = jnp.sum(weights, axis=1, keepdims=True)
        summed = jnp.dot(weights.astype(BF16), values[r], preferred_element_type=F32)
        some = mass > 0.0
        safe = jnp.where(some, mass, 1.0)
        mean = summed / safe
        log_mass = jnp.where(some, top + jnp.log(safe), NEG)
        o_wide[0, own, :] = mean[:, :LANES]
        o_wide[1, own, :] = mean[:, LANES:]
        o_wide[2, own, :] = jnp.broadcast_to(log_mass, (H, LANES))
        return carry

    lax.fori_loop(0, ROWS, attend, 0, unroll=UNROLL)

    def pack(n, carry):
        j = peer(lax.rem(n, 16), 1 - lax.div(n, 16))
        rows = pl.ds(pl.multiple_of(j * 2 * ROWS, 2 * ROWS), 2 * ROWS)
        s4[j, :, :LANES] = o_wide[0, rows, :].astype(BF16)
        s4[j, :, LANES:HD] = o_wide[1, rows, :].astype(BF16)
        log_mass = o_wide[2, rows, :]
        high = log_mass.astype(BF16).astype(F32)
        rest = log_mass - high
        middle = rest.astype(BF16).astype(F32)
        low = rest - middle
        lane = lane_of(log_mass.shape)
        s4[j, :, HD:] = jnp.where(lane == 0, high, jnp.where(lane == 1, middle, low)).astype(BF16)

        @pl.when(n < N_DEV - 1)
        def _():
            send(3, s4.at[j], r4.at[d], p, j)

        return carry

    lax.fori_loop(0, N_DEV, pack, 0)
    r4[d] = s4[d]
    landed(recv_sem, 3, r4, N_DEV - 1)

    pieces = r4[:, :, HD:].astype(F32)
    log_all = jnp.sum(jnp.where(lane_of(pieces.shape) < 3, pieces, 0.0), axis=2, keepdims=True)
    top_all = jnp.maximum(jnp.max(log_all, axis=0), score_new)
    share = jnp.exp(log_all - top_all[None])
    fresh = jnp.exp(score_new - top_all)
    mass_all = jnp.sum(share, axis=0) + fresh
    numerator = jnp.sum(share * r4[:, :, :HD].astype(F32), axis=0)
    numerator = numerator + fresh.astype(BF16).astype(F32) * value_new
    attended = numerator / mass_all
    own_heads = jnp.concatenate([attended[:ROWS], attended[ROWS:]], axis=1).astype(BF16)

    f_out.wait()

    def group_at(i):
        return lax.rem(x + entry(FAR_GROUP_X, i), 4) * 2 + lax.rem(lax.div(y, 2) + entry(FAR_GROUP_Y, i), 2)

    def columns_of(g):
        return pl.ds(pl.multiple_of(g * GROUP_COLS, LANES), GROUP_COLS)

    def chunks_of(block):
        return tiles_to_chunks([block[:, t * LANES : (t + 1) * LANES] for t in range(GROUP_COLS // LANES)])

    def project(i, carry):
        g = group_at(i)
        block = jnp.dot(own_heads, w_out[:, columns_of(g)], preferred_element_type=F32)
        for c, halves in enumerate(chunks_of(block)):
            j = g * GROUP + c
            s5[j] = jnp.concatenate(halves, axis=0).astype(BF16)

            @pl.when(j != d)
            def _():
                send(4, s5.at[j], r5.at[d], p, j)

        return carry

    lax.fori_loop(0, N_GROUP, project, 0)
    r5[d] = s5[d]

    turn = lax.rem(d * (COLS % LANES), LANES)
    back = lax.rem(LANES - turn, LANES)
    f_post_gain.wait()
    pad_gain[:, :COLS] = post_gain_v[...]
    lane = lane_of((ROWS, LANES))

    def unrotated(total):
        low_half = pltpu.roll(total[:ROWS], back, 1)
        high_half = pltpu.roll(total[ROWS:], back, 1)
        return low_half, jnp.where(lane < COLS - LANES, high_half, 0.0)

    landed(recv_sem, 4, r5, N_DEV - 1)
    attn_low, attn_high = unrotated(jnp.sum(r5[...].astype(F32), axis=0))
    res_low = pad_hidden[:, :LANES] + attn_low
    res_high = pad_hidden[:, LANES:] + attn_high
    row_squares = jnp.sum(res_low * res_low + res_high * res_high, axis=1, keepdims=True)
    coarse = row_squares.astype(BF16).astype(F32)
    fine = row_squares - coarse
    gained_low = res_low * pad_gain[:, :LANES]
    gained_high = res_high * pad_gain[:, LANES:]
    gained_high = jnp.where(lane == 96, coarse, jnp.where(lane == 97, fine, gained_high))
    tile = jnp.concatenate([pltpu.roll(gained_low, turn, 1), pltpu.roll(gained_high, turn, 1)], axis=0).astype(BF16)
    s6[...] = tile
    own = d * 2 + z_low
    r6[own] = tile

    def send_rows(n, carry):
        send(5, s6, r6.at[own], *peer_all(n))
        return carry

    lax.fori_loop(0, N_HALF - 1, send_rows, 0)
    landed(recv_sem, 5, r6, N_HALF - 1)

    some_rows = 2 * ROWS

    def assemble(g, sums):
        first = pl.multiple_of(g * 2 * GROUP, 2 * GROUP)
        block = r6[pl.ds(first, 2 * GROUP)].astype(F32).reshape(GROUP, 2, 2, ROWS, LANES)
        chunks = [
            (block[c, :, 0].reshape(some_rows, LANES), block[c, :, 1].reshape(some_rows, LANES))
            for c in range(GROUP)
        ]
        x_all[:, columns_of(g)] = jnp.concatenate(chunks_to_tiles(chunks), axis=1).astype(BF16)
        return tuple(total + chunk[1] for total, chunk in zip(sums, chunks))

    zeros = jnp.zeros((some_rows, LANES), F32)
    sums = lax.fori_loop(0, N_GROUP, assemble, (zeros,) * GROUP)
    lane_all = lane_of((some_rows, LANES))
    squares_at = zeros
    for c in range(GROUP):
        at = (96 + c * (COLS % LANES)) % LANES
        squares_at = squares_at + jnp.where((lane_all == at) | (lane_all == at + 1), sums[c], 0.0)
    all_squares = jnp.sum(squares_at, axis=1, keepdims=True)
    norm = lax.rsqrt(all_squares * (1.0 / D) + EPS)

    f_gate.wait()
    f_up.wait()
    shared[0].wait_recv()
    shared[1].wait_recv()
    transposed = (((1,), (1,)), ((), ()))

    def hidden_units(weights):
        units = weights[...].reshape(2 * weights.shape[1], D)
        return lax.dot_general(units, x_all[...], transposed, preferred_element_type=F32).T * norm

    gate = hidden_units(w_gate)
    up = hidden_units(w_up)
    activated = (gate / (1.0 + jnp.exp(-gate)) * up).astype(BF16)

    f_down.wait()
    shared[2].wait_recv()

    def pass_on(i, carry):
        g = group_at(i)
        columns = columns_of(g)
        weights = w_down[:, :, columns].reshape(2 * w_down.shape[1], GROUP_COLS)
        block = jnp.dot(activated, weights, preferred_element_type=F32)
        for c, (low_half, high_half) in enumerate(chunks_of(block)):
            for q in range(2):
                rows = slice(q * ROWS, (q + 1) * ROWS)
                at = (g * GROUP + c) * 2 + q
                s7[at] = jnp.concatenate([low_half[rows], high_half[rows]], axis=0).astype(BF16)

                @pl.when(at != own)
                def _():
                    send(9, s7.at[at], r7.at[own], q * 2 + core, g * GROUP + c)

        return carry

    lax.fori_loop(0, N_GROUP, pass_on, 0)
    r7[own] = s7[own]
    landed(recv_sem, 9, r7, N_HALF - 1)
    ffn_low, ffn_high = unrotated(jnp.sum(r7[...].astype(F32), axis=0))
    out_ref[:, :LANES] = res_low + ffn_low
    out_ref[:, LANES:] = (res_high + ffn_high)[:, : COLS - LANES]

    @pl.when(plane < EXTRA)
    def _():
        landed(send_sem, 0, s1, PLANE - 1 + EXTRA - 1)
        landed(send_sem, 1, r2, 2 * (N_DEV - 1))

    @pl.when(plane >= EXTRA)
    def _():
        landed(send_sem, 0, s1, PLANE - 1 + EXTRA)
        landed(send_sem, 1, r2, N_DEV - 1)

    landed(send_sem, 2, r3, N_DEV - 1)
    landed(send_sem, 3, r4, N_DEV - 1)
    landed(send_sem, 4, r5, N_DEV - 1)
    landed(send_sem, 5, r6, N_HALF - 1)
    for copy in shared:
        copy.wait_send()
    landed(send_sem, 9, r7, N_HALF - 1)


def local(
    hidden_in, in_gain, w_latent, q_gain, w_query, cache_keys, cache_values, lengths, w_out, post_gain,
    w_gate, w_up, w_down,
):
    operands = (
        hidden_in, in_gain[None, :], w_latent, q_gain[None, :], w_query, cache_keys, cache_values, lengths,
        w_out, post_gain[None, :], w_gate.T, w_up.T, w_down,
    )
    tile = (2 * ROWS, LANES)

    def like(array):
        return pltpu.VMEM(array.shape, array.dtype)

    scratch = [
        like(hidden_in),
        pltpu.VMEM((1, COLS), F32),
        pltpu.VMEM((1, QR), F32),
        pltpu.VMEM((1, COLS), F32),
        pltpu.SMEM(lengths.shape, jnp.int32),
        like(w_latent),
        like(w_query),
        like(cache_keys),
        like(cache_values),
        like(w_out),
        pltpu.VMEM((2, *w_gate.shape[::-1]), BF16),
        pltpu.VMEM((2, *w_up.shape[::-1]), BF16),
        pltpu.VMEM((2, *w_down.shape), BF16),
        pltpu.VMEM((ROWS, 2 * LANES), F32),
        pltpu.VMEM((1, 2 * LANES), F32),
        pltpu.VMEM((2 * PLANE, ROWS, LANES), F32),
        pltpu.VMEM((2 * PLANE, ROWS, LANES), F32),
        pltpu.VMEM((2, ROWS, LANES), F32),
        pltpu.VMEM((2 * N_DEV, ROWS, LANES), F32),
        pltpu.VMEM((2 * ROWS, HD), BF16),
        pltpu.VMEM((N_DEV, 2 * ROWS, HD), BF16),
        pltpu.VMEM((HD // LANES, H * ROWS, LANES), F32),
        pltpu.VMEM((MSG // LANES, H * ROWS, LANES), F32),
        pltpu.VMEM((N_DEV, 2 * ROWS, MSG), BF16),
        pltpu.VMEM((N_DEV, 2 * ROWS, MSG), BF16),
        pltpu.VMEM((N_DEV, *tile), BF16),
        pltpu.VMEM((N_DEV, *tile), BF16),
        pltpu.VMEM(tile, BF16),
        pltpu.VMEM((N_HALF, *tile), BF16),
        pltpu.VMEM((2 * ROWS, D), BF16),
        pltpu.VMEM((N_HALF, *tile), BF16),
        pltpu.VMEM((N_HALF, *tile), BF16),
        pltpu.VMEM((ROWS, HD, POS), BF16),
        pltpu.SemaphoreType.DMA((13,)),
        pltpu.SemaphoreType.DMA((10,)),
        pltpu.SemaphoreType.DMA((10,)),
    ]
    return pl.pallas_call(
        kernel,
        out_shape=pltpu.VMEM(hidden_in.shape, F32),
        in_specs=[pl.BlockSpec(memory_space=pl.ANY)] * len(operands),
        out_specs=pl.BlockSpec(memory_space=pltpu.VMEM),
        scratch_shapes=scratch,
        compiler_params=pltpu.CompilerParams(
            collective_id=0, has_side_effects=True, vmem_limit_bytes=56 * 2**20
        ),
    )(*operands)


def solution(mesh):
    placed = (
        P("pool", "dev"),
        P("dev"),
        P("dev", None),
        P(),
        P(None, "dev"),
        P("pool", "dev", None),
        P("pool", "dev", None),
        P("pool"),
        P("dev", None),
        P("dev"),
        P(None, ("pool", "dev")),
        P(None, ("pool", "dev")),
        P(("pool", "dev"), None),
    )
    return jax.shard_map(
        local, mesh=mesh, in_specs=placed, out_specs=P("pool", "dev"), check_vma=False
    )
```

```python
import math

import jax
import jax.numpy as jnp
from jax import lax
from jax.experimental import pallas as pl
from jax.experimental.pallas import tpu as pltpu
from jax.sharding import PartitionSpec as P

D = 7168
H = 64
HD = 256
QR = 2048
EPS = 1e-05
NEG = -1e30
MESH = pl.DeviceIdType.MESH

N_POOL = 4
N_DEV = 32
N_HALF = 2 * N_DEV
ROWS = 8
COLS = 224
LANES = 128
GROUP = 4
GROUP_COLS = GROUP * COLS
N_GROUP = N_DEV // GROUP
POS = 512
MSG = HD + LANES
UNROLL = 8

F32 = jnp.float32
BF16 = jnp.bfloat16


def lane_of(shape):
    return lax.broadcasted_iota(jnp.int32, shape, len(shape) - 1)


def tiles_to_chunks(tiles):
    lane = lane_of(tiles[0].shape)
    t = tiles
    return (
        (t[0], t[1]),
        (jnp.where(lane < 96, t[2], t[1]), jnp.where(lane < 96, t[3], t[2])),
        (jnp.where(lane < 64, t[4], t[3]), jnp.where(lane < 64, t[5], t[4])),
        (jnp.where(lane < 32, t[6], t[5]), t[6]),
    )


def chunks_to_tiles(chunks):
    (a0, b0), (a1, b1), (a2, b2), (a3, b3) = chunks
    lane = lane_of(a0.shape)
    return (
        a0,
        jnp.where(lane < 96, b0, a1),
        jnp.where(lane < 96, a1, b1),
        jnp.where(lane < 64, b1, a2),
        jnp.where(lane < 64, a2, b2),
        jnp.where(lane < 32, b2, a3),
        jnp.where(lane < 32, a3, b3),
    )


def packed(values, bits):
    word = sum(value << (bits * k) for k, value in enumerate(values))
    return word - 2**32 if word >= 2**31 else word


FAR = ((2, 2), (2, 1), (1, 2), (2, 3), (3, 2), (1, 1), (3, 3), (1, 3), (3, 1), (2, 0), (0, 2), (1, 0), (0, 1), (3, 0), (0, 3), (0, 0))
FAR_X = packed([step[0] for step in FAR], 2)
FAR_Y = packed([step[1] for step in FAR], 2)
FAR_GROUP_X = packed([2, 2, 1, 3, 1, 3, 0, 0], 2)
FAR_GROUP_Y = packed([1, 0, 1, 1, 0, 0, 1, 0], 2)
PLANE = 16
N_LINE = 4
SCALE_INV = 1.0 / math.sqrt(HD)


def entry(word, k):
    return lax.bitwise_and(lax.shift_right_logical(jnp.int32(word), 2 * k), 3)


def kernel(
    hidden_hbm, in_gain_hbm, w_latent_hbm, q_gain_hbm, w_query_hbm, keys_hbm, values_hbm, lengths_hbm,
    w_out_hbm, post_gain_hbm, w_gate_hbm, w_up_hbm, w_down_hbm,
    out_ref,
    hidden_v, in_gain_v, q_gain_v, post_gain_v, lengths, w_latent, w_query, keys, values, w_out, w_gate, w_up, w_down,
    pad_hidden, pad_gain, s1, r1, s2, r2, s2_new, r2_new, s2_squares, r2_squares, sent_rows, s3, r3, q_wide, o_wide, s4, r4, s5, r5, s6, r6, x_all, s7, r7, keys_t,
    local_sem, send_sem, recv_sem, wave_sem,
):
    p = lax.axis_index("pool")
    d = lax.axis_index("dev")
    x = lax.div(d, 8)
    y = lax.rem(lax.div(d, 2), 4)
    z_high = lax.rem(d, 2)
    z_low = lax.div(p, 2)
    core = lax.rem(p, 2)
    sibling = z_low * 2 + 1 - core

    def peer(i, dz):
        there = lax.rem(x + entry(FAR_X, i), 4) * 8 + lax.rem(y + entry(FAR_Y, i), 4) * 2
        return there + lax.rem(z_high + dz, 2)

    def peer_all(n):
        part = lax.rem(n, 4)
        there = peer(lax.div(n, 4), 1 - lax.div(part, 2))
        return lax.rem(z_low + lax.rem(lax.div(part + 1, 2), 2), 2) * 2 + core, there

    def fetch(i, source, target):
        copy = pltpu.make_async_copy(source, target, local_sem.at[i])
        copy.start()
        return copy

    f_hidden = fetch(0, hidden_hbm, hidden_v)
    f_in_gain = fetch(1, in_gain_hbm, in_gain_v)
    f_latent = fetch(2, w_latent_hbm, w_latent)

    barrier = pltpu.get_barrier_semaphore()

    def moved(dx, dy):
        return lax.rem(x + dx, 4) * 8 + lax.rem(y + dy, 4) * 2 + z_high

    across = 2 * (1 - z_low) + core
    other = peer(PLANE - 1, 1)
    x_line = [(p, moved(step, 0)) for step in (2, 1, 3)]
    y_line = [(p, moved(0, step)) for step in (2, 1, 3)]
    z_column = [(p, other), (across, other), (across, d)]

    def signal(semaphore, devices):
        for device in devices:
            pl.semaphore_signal(semaphore, inc=1, device_id=device, device_id_type=MESH)

    signal(barrier, x_line + y_line + z_column + [(sibling, d)])

    f_q_gain = fetch(3, q_gain_hbm, q_gain_v)
    f_query = fetch(4, w_query_hbm, w_query)
    f_keys = fetch(5, keys_hbm, keys)
    f_lengths = fetch(6, lengths_hbm, lengths)
    f_values = fetch(7, values_hbm, values)
    f_out = fetch(8, w_out_hbm, w_out)
    f_post_gain = fetch(9, post_gain_hbm, post_gain_v)
    f_gate = fetch(10, w_gate_hbm, w_gate.at[0])
    f_up = fetch(11, w_up_hbm, w_up.at[0])
    f_down = fetch(12, w_down_hbm, w_down.at[0])

    def remote(i, source, target, pool, dev):
        return pltpu.make_async_remote_copy(
            src_ref=source,
            dst_ref=target,
            send_sem=send_sem.at[i],
            recv_sem=recv_sem.at[i],
            device_id=(pool, dev),
            device_id_type=MESH,
        )

    def send(*args):
        remote(*args).start()

    def landed(sem, i, ref, count):
        block = ref.at[pl.ds(0, count)]
        pltpu.make_async_copy(block, block, sem.at[i]).wait()

    def to_group(i, source, target):
        def step(n, carry):
            send(i, source, target, p, peer(lax.rem(n, 16), 1 - lax.div(n, 16)))
            return carry

        lax.fori_loop(0, N_DEV - 1, step, 0)

    pad_hidden[...] = jnp.zeros_like(pad_hidden)
    pad_gain[...] = jnp.zeros_like(pad_gain)
    f_hidden.wait()
    f_in_gain.wait()
    hidden_f = hidden_v[...].astype(F32)
    pad_hidden[:, :COLS] = hidden_f
    square_part = jnp.sum(hidden_f * hidden_f, axis=1, keepdims=True)
    scaled_in = (hidden_f * in_gain_v[...]).astype(BF16)
    f_latent.wait()
    part = jnp.dot(scaled_in, w_latent[...], preferred_element_type=F32)
    coarse = square_part.astype(BF16).astype(F32)
    squares_pair = jnp.where(lane_of((ROWS, LANES)) < LANES // 2, coarse, square_part - coarse)
    for owner in range(N_LINE):
        firsts = [4 * owner, 4 * owner + 1, 4 * owner + 2, 4 * owner + 3, QR // LANES + owner]
        pieces = [part[:, c * LANES : (c + 1) * LANES] for c in firsts] + [squares_pair]
        s1[owner] = jnp.concatenate(pieces, axis=0).astype(BF16)

    pl.semaphore_wait(barrier, len(x_line + y_line + z_column) + 1)

    for device in x_line:
        send(0, s1.at[lax.div(device[1], 8)], r1.at[x], *device)
    signal(wave_sem.at[0], z_column)

    shared = [
        remote(6 + k, source, target.at[1], sibling, d)
        for k, (source, target) in enumerate(((w_gate_hbm, w_gate), (w_up_hbm, w_up), (w_down_hbm, w_down)))
    ]
    for copy in shared:
        copy.start()

    pl.semaphore_wait(wave_sem.at[0], len(z_column))
    signal(wave_sem.at[1], x_line)

    r1[x] = s1[x]
    landed(recv_sem, 0, r1, N_LINE - 1)
    line_sum = jnp.sum(r1[...].astype(F32), axis=0)
    query_part = line_sum[: 4 * ROWS].astype(BF16)
    s2[...] = query_part
    r2[d] = query_part
    s2_new[...] = line_sum[4 * ROWS :].astype(BF16)
    r2_new[d] = line_sum[4 * ROWS :].astype(BF16)
    pair_sum = line_sum[5 * ROWS :]
    squares_line = pair_sum + pltpu.roll(pair_sum, LANES // 2, 1)
    diagonal = lane_of((ROWS, LANES)) == lax.broadcasted_iota(jnp.int32, (ROWS, LANES), 0)
    squares_row = jnp.sum(jnp.where(diagonal, squares_line, 0.0), axis=0, keepdims=True)
    s2_squares[...] = squares_row
    place = lax.rem(d, 8)
    gives_squares = x == lax.rem(place, N_LINE)

    pl.semaphore_wait(wave_sem.at[1], len(x_line))

    @pl.when(gives_squares)
    def _():
        r2_squares[place] = squares_row
        to_group(11, s2_squares, r2_squares.at[place])

    to_group(1, s2, r2.at[d])
    f_keys.wait()

    def turn_keys(r, carry):
        keys_t[r] = keys[r].T
        return carry

    lax.fori_loop(0, ROWS, turn_keys, 0)

    @pl.when(gives_squares)
    def _():
        landed(recv_sem, 11, r2_squares, 7)

    @pl.when(jnp.logical_not(gives_squares))
    def _():
        landed(recv_sem, 11, r2_squares, 8)

    landed(recv_sem, 1, r2, N_DEV - 1)

    squares_all = jnp.where(diagonal, jnp.sum(r2_squares[...], axis=0), 0.0)
    row_scale = lax.rsqrt(jnp.sum(squares_all, axis=1, keepdims=True) * (1.0 / D) + EPS)
    latents = []
    for owner in range(N_LINE):
        chunk = jnp.sum(r2[8 * owner : 8 * owner + 8].astype(F32), axis=0)
        latents += [chunk[c * ROWS : (c + 1) * ROWS] * row_scale for c in range(4)]
    squares = latents[0] * latents[0]
    for c in range(1, QR // LANES):
        squares = squares + latents[c] * latents[c]
    latent_mean = jnp.sum(squares, axis=1, keepdims=True) * (1.0 / QR)
    query_latent = jnp.concatenate(latents, axis=1)
    f_q_gain.wait()
    query_normed = (query_latent * lax.rsqrt(latent_mean + EPS) * q_gain_v[...]).astype(BF16)
    f_query.wait()
    query = jnp.dot(query_normed, w_query[...], preferred_element_type=F32)
    query_rows = jnp.concatenate([query[:, :HD], query[:, HD:]], axis=0).astype(BF16)
    s3[...] = query_rows
    r3[d] = query_rows
    to_group(2, s3, r3.at[d])

    to_group(10, s2_new, r2_new.at[d])

    f_lengths.wait()
    f_values.wait()
    landed(recv_sem, 2, r3, N_DEV - 1)
    q_all = r3[...].reshape(N_DEV * 2 * ROWS, HD).astype(F32)
    q_wide[0] = q_all[:, :LANES]
    q_wide[1] = q_all[:, LANES:]

    def attend(r, carry):
        own = pl.ds(r, H, stride=ROWS)
        q = jnp.concatenate([q_wide[0, own, :], q_wide[1, own, :]], axis=1).astype(BF16)
        scores = jnp.dot(q, keys_t[r], preferred_element_type=F32) * SCALE_INV
        position = d * POS + lax.broadcasted_iota(jnp.int32, (H, POS), 1)
        valid = position < lengths[r]
        masked = jnp.where(valid, scores, NEG)
        top = jnp.max(masked, axis=1, keepdims=True)
        weights = jnp.where(valid, jnp.exp(masked - top), 0.0)
        mass = jnp.sum(weights, axis=1, keepdims=True)
        summed = jnp.dot(weights.astype(BF16), values[r], preferred_element_type=F32)
        some = mass > 0.0
        safe = jnp.where(some, mass, 1.0)
        mean = summed / safe
        log_mass = jnp.where(some, top + jnp.log(safe), NEG)
        o_wide[0, own, :] = mean[:, :LANES]
        o_wide[1, own, :] = mean[:, LANES:]
        o_wide[2, own, :] = jnp.broadcast_to(log_mass, (H, LANES))
        return carry

    lax.fori_loop(0, ROWS, attend, 0, unroll=UNROLL)

    def pack(n, carry):
        j = peer(lax.rem(n, 16), 1 - lax.div(n, 16))
        rows = pl.ds(pl.multiple_of(j * 2 * ROWS, 2 * ROWS), 2 * ROWS)
        s4[j, :, :LANES] = o_wide[0, rows, :].astype(BF16)
        s4[j, :, LANES:HD] = o_wide[1, rows, :].astype(BF16)
        log_mass = o_wide[2, rows, :]
        high = log_mass.astype(BF16).astype(F32)
        rest = log_mass - high
        middle = rest.astype(BF16).astype(F32)
        low = rest - middle
        lane = lane_of(log_mass.shape)
        s4[j, :, HD:] = jnp.where(lane == 0, high, jnp.where(lane == 1, middle, low)).astype(BF16)

        @pl.when(n < N_DEV - 1)
        def _():
            send(3, s4.at[j], r4.at[d], p, j)

        return carry

    lax.fori_loop(0, N_DEV, pack, 0)
    r4[d] = s4[d]

    landed(recv_sem, 10, r2_new, N_DEV - 1)

    def wide_new(first):
        new = [
            jnp.sum(r2_new[8 * owner : 8 * owner + 8, :ROWS].astype(F32), axis=0) * row_scale
            for owner in (first, first + 1)
        ]
        new = jnp.concatenate(new, axis=1).astype(BF16).astype(F32)
        return jnp.concatenate([new, new], axis=0)

    key_new = wide_new(0)
    value_new = wide_new(2)
    score_new = jnp.sum(query_rows.astype(F32) * key_new, axis=1, keepdims=True) * SCALE_INV

    landed(recv_sem, 3, r4, N_DEV - 1)

    pieces = r4[:, :, HD:].astype(F32)
    log_all = jnp.sum(jnp.where(lane_of(pieces.shape) < 3, pieces, 0.0), axis=2, keepdims=True)
    top_all = jnp.maximum(jnp.max(log_all, axis=0), score_new)
    share = jnp.exp(log_all - top_all[None])
    fresh = jnp.exp(score_new - top_all)
    mass_all = jnp.sum(share, axis=0) + fresh
    numerator = jnp.sum(share * r4[:, :, :HD].astype(F32), axis=0)
    numerator = numerator + fresh.astype(BF16).astype(F32) * value_new
    attended = numerator / mass_all
    own_heads = jnp.concatenate([attended[:ROWS], attended[ROWS:]], axis=1).astype(BF16)

    f_out.wait()

    def group_at(i):
        return lax.rem(x + entry(FAR_GROUP_X, i), 4) * 2 + lax.rem(lax.div(y, 2) + entry(FAR_GROUP_Y, i), 2)

    def columns_of(g):
        return pl.ds(pl.multiple_of(g * GROUP_COLS, LANES), GROUP_COLS)

    def chunks_of(block):
        return tiles_to_chunks([block[:, t * LANES : (t + 1) * LANES] for t in range(GROUP_COLS // LANES)])

    def project(i, carry):
        g = group_at(i)
        block = jnp.dot(own_heads, w_out[:, columns_of(g)], preferred_element_type=F32)
        for c, halves in enumerate(chunks_of(block)):
            j = g * GROUP + c
            s5[j] = jnp.concatenate(halves, axis=0).astype(BF16)

            @pl.when(j != d)
            def _():
                send(4, s5.at[j], r5.at[d], p, j)

        return carry

    lax.fori_loop(0, N_GROUP, project, 0)
    r5[d] = s5[d]

    turn = lax.rem(d * (COLS % LANES), LANES)
    back = lax.rem(LANES - turn, LANES)
    f_post_gain.wait()
    pad_gain[:, :COLS] = post_gain_v[...]
    lane = lane_of((ROWS, LANES))

    def unrotated(total):
        low_half = pltpu.roll(total[:ROWS], back, 1)
        high_half = pltpu.roll(total[ROWS:], back, 1)
        return low_half, jnp.where(lane < COLS - LANES, high_half, 0.0)

    landed(recv_sem, 4, r5, N_DEV - 1)
    attn_low, attn_high = unrotated(jnp.sum(r5[...].astype(F32), axis=0))
    res_low = pad_hidden[:, :LANES] + attn_low
    res_high = pad_hidden[:, LANES:] + attn_high
    row_squares = jnp.sum(res_low * res_low + res_high * res_high, axis=1, keepdims=True)
    coarse = row_squares.astype(BF16).astype(F32)
    fine = row_squares - coarse
    gained_low = res_low * pad_gain[:, :LANES]
    gained_high = res_high * pad_gain[:, LANES:]
    gained_high = jnp.where(lane == 96, coarse, jnp.where(lane == 97, fine, gained_high))
    tile = jnp.concatenate([pltpu.roll(gained_low, turn, 1), pltpu.roll(gained_high, turn, 1)], axis=0).astype(BF16)
    s6[...] = tile
    own = d * 2 + z_low
    r6[own] = tile

    def send_rows(n, carry):
        send(5, s6, r6.at[own], *peer_all(n))
        return carry

    lax.fori_loop(0, N_HALF - 1, send_rows, 0)
    landed(recv_sem, 5, r6, N_HALF - 1)

    some_rows = 2 * ROWS

    def assemble(g, sums):
        first = pl.multiple_of(g * 2 * GROUP, 2 * GROUP)
        block = r6[pl.ds(first, 2 * GROUP)].astype(F32).reshape(GROUP, 2, 2, ROWS, LANES)
        chunks = [
            (block[c, :, 0].reshape(some_rows, LANES), block[c, :, 1].reshape(some_rows, LANES))
            for c in range(GROUP)
        ]
        x_all[:, columns_of(g)] = jnp.concatenate(chunks_to_tiles(chunks), axis=1).astype(BF16)
        return tuple(total + chunk[1] for total, chunk in zip(sums, chunks))

    zeros = jnp.zeros((some_rows, LANES), F32)
    sums = lax.fori_loop(0, N_GROUP, assemble, (zeros,) * GROUP)
    lane_all = lane_of((some_rows, LANES))
    squares_at = zeros
    for c in range(GROUP):
        at = (96 + c * (COLS % LANES)) % LANES
        squares_at = squares_at + jnp.where((lane_all == at) | (lane_all == at + 1), sums[c], 0.0)
    all_squares = jnp.sum(squares_at, axis=1, keepdims=True)
    norm = lax.rsqrt(all_squares * (1.0 / D) + EPS)

    f_gate.wait()
    f_up.wait()
    shared[0].wait_recv()
    shared[1].wait_recv()
    transposed = (((1,), (1,)), ((), ()))

    def hidden_units(weights):
        units = weights[...].reshape(2 * weights.shape[1], D)
        return lax.dot_general(units, x_all[...], transposed, preferred_element_type=F32).T * norm

    gate = hidden_units(w_gate)
    up = hidden_units(w_up)
    activated = (gate / (1.0 + jnp.exp(-gate)) * up).astype(BF16)

    f_down.wait()
    shared[2].wait_recv()

    def pass_on(i, carry):
        g = group_at(i)
        columns = columns_of(g)
        weights = w_down[:, :, columns].reshape(2 * w_down.shape[1], GROUP_COLS)
        block = jnp.dot(activated, weights, preferred_element_type=F32)
        for c, (low_half, high_half) in enumerate(chunks_of(block)):
            for q in range(2):
                rows = slice(q * ROWS, (q + 1) * ROWS)
                at = (g * GROUP + c) * 2 + q
                s7[at] = jnp.concatenate([low_half[rows], high_half[rows]], axis=0).astype(BF16)

                @pl.when(at != own)
                def _():
                    send(9, s7.at[at], r7.at[own], q * 2 + core, g * GROUP + c)

        return carry

    lax.fori_loop(0, N_GROUP, pass_on, 0)
    r7[own] = s7[own]
    landed(recv_sem, 9, r7, N_HALF - 1)
    ffn_low, ffn_high = unrotated(jnp.sum(r7[...].astype(F32), axis=0))
    out_ref[:, :LANES] = res_low + ffn_low
    out_ref[:, LANES:] = (res_high + ffn_high)[:, : COLS - LANES]

    @pl.when(gives_squares)
    def _():
        landed(send_sem, 11, sent_rows, N_DEV - 1)

    landed(send_sem, 0, r1, N_LINE - 1)
    landed(send_sem, 1, r2, N_DEV - 1)
    landed(send_sem, 10, r2_new, N_DEV - 1)
    landed(send_sem, 2, r3, N_DEV - 1)
    landed(send_sem, 3, r4, N_DEV - 1)
    landed(send_sem, 4, r5, N_DEV - 1)
    landed(send_sem, 5, r6, N_HALF - 1)
    for copy in shared:
        copy.wait_send()
    landed(send_sem, 9, r7, N_HALF - 1)


def local(
    hidden_in, in_gain, w_latent, q_gain, w_query, cache_keys, cache_values, lengths, w_out, post_gain,
    w_gate, w_up, w_down,
):
    operands = (
        hidden_in, in_gain[None, :], w_latent, q_gain[None, :], w_query, cache_keys, cache_values, lengths,
        w_out, post_gain[None, :], w_gate.T, w_up.T, w_down,
    )
    tile = (2 * ROWS, LANES)

    def like(array):
        return pltpu.VMEM(array.shape, array.dtype)

    scratch = [
        like(hidden_in),
        pltpu.VMEM((1, COLS), F32),
        pltpu.VMEM((1, QR), F32),
        pltpu.VMEM((1, COLS), F32),
        pltpu.SMEM(lengths.shape, jnp.int32),
        like(w_latent),
        like(w_query),
        like(cache_keys),
        like(cache_values),
        like(w_out),
        pltpu.VMEM((2, *w_gate.shape[::-1]), BF16),
        pltpu.VMEM((2, *w_up.shape[::-1]), BF16),
        pltpu.VMEM((2, *w_down.shape), BF16),
        pltpu.VMEM((ROWS, 2 * LANES), F32),
        pltpu.VMEM((1, 2 * LANES), F32),
        pltpu.VMEM((N_LINE, 6 * ROWS, LANES), BF16),
        pltpu.VMEM((N_LINE, 6 * ROWS, LANES), BF16),
        pltpu.VMEM((4 * ROWS, LANES), BF16),
        pltpu.VMEM((N_DEV, 4 * ROWS, LANES), BF16),
        pltpu.VMEM(tile, BF16),
        pltpu.VMEM((N_DEV, *tile), BF16),
        pltpu.VMEM((1, LANES), F32),
        pltpu.VMEM((8, 1, LANES), F32),
        pltpu.VMEM((N_DEV, 1, LANES), F32),
        pltpu.VMEM((2 * ROWS, HD), BF16),
        pltpu.VMEM((N_DEV, 2 * ROWS, HD), BF16),
        pltpu.VMEM((HD // LANES, H * ROWS, LANES), F32),
        pltpu.VMEM((MSG // LANES, H * ROWS, LANES), F32),
        pltpu.VMEM((N_DEV, 2 * ROWS, MSG), BF16),
        pltpu.VMEM((N_DEV, 2 * ROWS, MSG), BF16),
        pltpu.VMEM((N_DEV, *tile), BF16),
        pltpu.VMEM((N_DEV, *tile), BF16),
        pltpu.VMEM(tile, BF16),
        pltpu.VMEM((N_HALF, *tile), BF16),
        pltpu.VMEM((2 * ROWS, D), BF16),
        pltpu.VMEM((N_HALF, *tile), BF16),
        pltpu.VMEM((N_HALF, *tile), BF16),
        pltpu.VMEM((ROWS, HD, POS), BF16),
        pltpu.SemaphoreType.DMA((13,)),
        pltpu.SemaphoreType.DMA((12,)),
        pltpu.SemaphoreType.DMA((12,)),
        pltpu.SemaphoreType.REGULAR((2,)),
    ]
    return pl.pallas_call(
        kernel,
        out_shape=pltpu.VMEM(hidden_in.shape, F32),
        in_specs=[pl.BlockSpec(memory_space=pl.ANY)] * len(operands),
        out_specs=pl.BlockSpec(memory_space=pltpu.VMEM),
        scratch_shapes=scratch,
        compiler_params=pltpu.CompilerParams(
            collective_id=0, has_side_effects=True, vmem_limit_bytes=56 * 2**20
        ),
    )(*operands)


def solution(mesh):
    placed = (
        P("pool", "dev"),
        P("dev"),
        P("dev", None),
        P(),
        P(None, "dev"),
        P("pool", "dev", None),
        P("pool", "dev", None),
        P("pool"),
        P("dev", None),
        P("dev"),
        P(None, ("pool", "dev")),
        P(None, ("pool", "dev")),
        P(("pool", "dev"), None),
    )
    return jax.shard_map(
        local, mesh=mesh, in_specs=placed, out_specs=P("pool", "dev"), check_vma=False
    )
```

```python
import math

import jax
import jax.numpy as jnp
from jax import lax
from jax.experimental import pallas as pl
from jax.experimental.pallas import tpu as pltpu
from jax.sharding import PartitionSpec as P

D = 7168
H = 64
HD = 256
QR = 2048
EPS = 1e-05
NEG = -1e30
MESH = pl.DeviceIdType.MESH

N_POOL = 4
N_DEV = 32
N_HALF = 2 * N_DEV
ROWS = 8
COLS = 224
LANES = 128
GROUP = 4
GROUP_COLS = GROUP * COLS
N_GROUP = N_DEV // GROUP
POS = 512
MSG = HD + LANES
UNROLL = 8

F32 = jnp.float32
BF16 = jnp.bfloat16


def lane_of(shape):
    return lax.broadcasted_iota(jnp.int32, shape, len(shape) - 1)


def tiles_to_chunks(tiles):
    lane = lane_of(tiles[0].shape)
    t = tiles
    return (
        (t[0], t[1]),
        (jnp.where(lane < 96, t[2], t[1]), jnp.where(lane < 96, t[3], t[2])),
        (jnp.where(lane < 64, t[4], t[3]), jnp.where(lane < 64, t[5], t[4])),
        (jnp.where(lane < 32, t[6], t[5]), t[6]),
    )


def chunks_to_tiles(chunks):
    (a0, b0), (a1, b1), (a2, b2), (a3, b3) = chunks
    lane = lane_of(a0.shape)
    return (
        a0,
        jnp.where(lane < 96, b0, a1),
        jnp.where(lane < 96, a1, b1),
        jnp.where(lane < 64, b1, a2),
        jnp.where(lane < 64, a2, b2),
        jnp.where(lane < 32, b2, a3),
        jnp.where(lane < 32, a3, b3),
    )


def packed(values, bits):
    word = sum(value << (bits * k) for k, value in enumerate(values))
    return word - 2**32 if word >= 2**31 else word


FAR = ((2, 2), (2, 1), (1, 2), (2, 3), (3, 2), (1, 1), (3, 3), (1, 3), (3, 1), (2, 0), (0, 2), (1, 0), (0, 1), (3, 0), (0, 3), (0, 0))
FAR_X = packed([step[0] for step in FAR], 2)
FAR_Y = packed([step[1] for step in FAR], 2)
FAR_GROUP_X = packed([2, 2, 1, 3, 1, 3, 0, 0], 2)
FAR_GROUP_Y = packed([1, 0, 1, 1, 0, 0, 1, 0], 2)
PLANE = 16
N_LINE = 4
SCALE_INV = 1.0 / math.sqrt(HD)


def entry(word, k):
    return lax.bitwise_and(lax.shift_right_logical(jnp.int32(word), 2 * k), 3)


def kernel(
    hidden_hbm, in_gain_hbm, w_latent_hbm, q_gain_hbm, w_query_hbm, keys_hbm, values_hbm, lengths_hbm,
    w_out_hbm, post_gain_hbm, w_gate_hbm, w_up_hbm, w_down_hbm,
    out_ref,
    hidden_v, in_gain_v, q_gain_v, post_gain_v, lengths, w_latent, w_query, keys, values, w_out, w_gate, w_up, w_down,
    pad_hidden, pad_gain, s1, r1, s2, r2, s2_new, r2_new, s3_new, r3_new, s2_squares, r2_squares, sent_rows, s3, r3, q_wide, o_wide, s4, r4, s4_mass, r4_mass, s5, r5, s6, r6, x_all, s7, r7, keys_t,
    local_sem, send_sem, recv_sem, wave_sem,
):
    p = lax.axis_index("pool")
    d = lax.axis_index("dev")
    x = lax.div(d, 8)
    y = lax.rem(lax.div(d, 2), 4)
    z_high = lax.rem(d, 2)
    z_low = lax.div(p, 2)
    core = lax.rem(p, 2)
    sibling = z_low * 2 + 1 - core

    def peer(i, dz):
        there = lax.rem(x + entry(FAR_X, i), 4) * 8 + lax.rem(y + entry(FAR_Y, i), 4) * 2
        return there + lax.rem(z_high + dz, 2)

    def peer_all(n):
        part = lax.rem(n, 4)
        there = peer(lax.div(n, 4), 1 - lax.div(part, 2))
        return lax.rem(z_low + lax.rem(lax.div(part + 1, 2), 2), 2) * 2 + core, there

    def fetch(i, source, target):
        copy = pltpu.make_async_copy(source, target, local_sem.at[i])
        copy.start()
        return copy

    f_hidden = fetch(0, hidden_hbm, hidden_v)
    f_in_gain = fetch(1, in_gain_hbm, in_gain_v)
    f_latent = fetch(2, w_latent_hbm, w_latent)

    barrier = pltpu.get_barrier_semaphore()

    def moved(dx, dy):
        return lax.rem(x + dx, 4) * 8 + lax.rem(y + dy, 4) * 2 + z_high

    across = 2 * (1 - z_low) + core
    other = peer(PLANE - 1, 1)
    x_line = [(p, moved(step, 0)) for step in (2, 1, 3)]
    y_line = [(p, moved(0, step)) for step in (2, 1, 3)]
    z_column = [(p, other), (across, other), (across, d)]

    def signal(semaphore, devices):
        for device in devices:
            pl.semaphore_signal(semaphore, inc=1, device_id=device, device_id_type=MESH)

    signal(barrier, x_line + y_line + z_column + [(sibling, d)])

    f_q_gain = fetch(3, q_gain_hbm, q_gain_v)
    f_query = fetch(4, w_query_hbm, w_query)
    f_keys = fetch(5, keys_hbm, keys)
    f_lengths = fetch(6, lengths_hbm, lengths)
    f_values = fetch(7, values_hbm, values)
    f_out = fetch(8, w_out_hbm, w_out)
    f_post_gain = fetch(9, post_gain_hbm, post_gain_v)
    f_gate = fetch(10, w_gate_hbm, w_gate.at[0])
    f_up = fetch(11, w_up_hbm, w_up.at[0])
    f_down = fetch(12, w_down_hbm, w_down.at[0])

    def remote(i, source, target, pool, dev):
        return pltpu.make_async_remote_copy(
            src_ref=source,
            dst_ref=target,
            send_sem=send_sem.at[i],
            recv_sem=recv_sem.at[i],
            device_id=(pool, dev),
            device_id_type=MESH,
        )

    def send(*args):
        remote(*args).start()

    def landed(sem, i, ref, count):
        block = ref.at[pl.ds(0, count)]
        pltpu.make_async_copy(block, block, sem.at[i]).wait()

    def to_group(i, source, target):
        def step(n, carry):
            send(i, source, target, p, peer(lax.rem(n, 16), 1 - lax.div(n, 16)))
            return carry

        lax.fori_loop(0, N_DEV - 1, step, 0, unroll=31)

    pad_hidden[...] = jnp.zeros_like(pad_hidden)
    pad_gain[...] = jnp.zeros_like(pad_gain)
    f_hidden.wait()
    f_in_gain.wait()
    hidden_f = hidden_v[...].astype(F32)
    pad_hidden[:, :COLS] = hidden_f
    square_part = jnp.sum(hidden_f * hidden_f, axis=1, keepdims=True)
    scaled_in = (hidden_f * in_gain_v[...]).astype(BF16)
    f_latent.wait()
    part = jnp.dot(scaled_in, w_latent[...], preferred_element_type=F32)
    coarse = square_part.astype(BF16).astype(F32)
    squares_pair = jnp.where(lane_of((ROWS, LANES)) < LANES // 2, coarse, square_part - coarse)
    for owner in range(N_LINE):
        firsts = [4 * owner, 4 * owner + 1, 4 * owner + 2, 4 * owner + 3, QR // LANES + owner]
        pieces = [part[:, c * LANES : (c + 1) * LANES] for c in firsts] + [squares_pair]
        s1[owner] = jnp.concatenate(pieces, axis=0).astype(BF16)

    pl.semaphore_wait(barrier, len(x_line + y_line + z_column) + 1)

    for device in x_line:
        send(0, s1.at[lax.div(device[1], 8)], r1.at[x], *device)
    signal(wave_sem.at[0], z_column)

    shared = [
        remote(6 + k, source, target.at[1], sibling, d)
        for k, (source, target) in enumerate(((w_gate_hbm, w_gate), (w_up_hbm, w_up), (w_down_hbm, w_down)))
    ]
    for copy in shared:
        copy.start()

    pl.semaphore_wait(wave_sem.at[0], len(z_column))
    signal(wave_sem.at[1], x_line)

    r1[x] = s1[x]
    landed(recv_sem, 0, r1, N_LINE - 1)
    line_sum = jnp.sum(r1[...].astype(F32), axis=0)
    query_part = line_sum[: 4 * ROWS].astype(BF16)
    s2[...] = query_part
    r2[d] = query_part
    s2_new[...] = line_sum[4 * ROWS :].astype(BF16)
    pair_sum = line_sum[5 * ROWS :]
    squares_line = pair_sum + pltpu.roll(pair_sum, LANES // 2, 1)
    diagonal = lane_of((ROWS, LANES)) == lax.broadcasted_iota(jnp.int32, (ROWS, LANES), 0)
    squares_row = jnp.sum(jnp.where(diagonal, squares_line, 0.0), axis=0, keepdims=True)
    s2_squares[...] = squares_row
    place = lax.rem(d, 8)
    adds_new = place == 2 * x
    gives_squares = x == lax.rem(place, N_LINE)

    pl.semaphore_wait(wave_sem.at[1], len(x_line))

    @pl.when(gives_squares)
    def _():
        r2_squares[place] = squares_row
        to_group(11, s2_squares, r2_squares.at[place])

    to_group(1, s2, r2.at[d])

    @pl.when(adds_new)
    def _():
        r2_new[place] = s2_new[...]

    @pl.when(jnp.logical_not(adds_new))
    def _():
        send(10, s2_new, r2_new.at[place], p, x * 8 + 2 * x)

    f_keys.wait()

    def turn_keys(r, carry):
        keys_t[r] = keys[r].T
        return carry

    lax.fori_loop(0, ROWS, turn_keys, 0)

    @pl.when(gives_squares)
    def _():
        landed(recv_sem, 11, r2_squares, 7)

    @pl.when(jnp.logical_not(gives_squares))
    def _():
        landed(recv_sem, 11, r2_squares, 8)

    landed(recv_sem, 1, r2, N_DEV - 1)

    squares_all = jnp.where(diagonal, jnp.sum(r2_squares[...], axis=0), 0.0)
    row_scale = lax.rsqrt(jnp.sum(squares_all, axis=1, keepdims=True) * (1.0 / D) + EPS)
    latents = []
    for owner in range(N_LINE):
        chunk = jnp.sum(r2[8 * owner : 8 * owner + 8].astype(F32), axis=0)
        latents += [chunk[c * ROWS : (c + 1) * ROWS] * row_scale for c in range(4)]
    squares = latents[0] * latents[0]
    for c in range(1, QR // LANES):
        squares = squares + latents[c] * latents[c]
    latent_mean = jnp.sum(squares, axis=1, keepdims=True) * (1.0 / QR)
    query_latent = jnp.concatenate(latents, axis=1)
    f_q_gain.wait()
    query_normed = (query_latent * lax.rsqrt(latent_mean + EPS) * q_gain_v[...]).astype(BF16)
    f_query.wait()
    query = jnp.dot(query_normed, w_query[...], preferred_element_type=F32)
    query_rows = jnp.concatenate([query[:, :HD], query[:, HD:]], axis=0).astype(BF16)
    s3[...] = query_rows
    r3[d] = query_rows
    to_group(2, s3, r3.at[d])

    @pl.when(adds_new)
    def _():
        landed(recv_sem, 10, r2_new, 7)
        total = jnp.sum(r2_new[...].astype(F32), axis=0)[:ROWS]
        coarse = total.astype(BF16).astype(F32)
        both = jnp.concatenate([coarse, total - coarse], axis=0).astype(BF16)
        s3_new[...] = both
        r3_new[x] = both
        to_group(13, s3_new, r3_new.at[x])

    f_lengths.wait()
    f_values.wait()
    landed(recv_sem, 2, r3, N_DEV - 1)
    q_all = r3[...].reshape(N_DEV * 2 * ROWS, HD).astype(F32)
    q_wide[0] = q_all[:, :LANES]
    q_wide[1] = q_all[:, LANES:]

    def attend(r, carry):
        own = pl.ds(r, H, stride=ROWS)
        q = jnp.concatenate([q_wide[0, own, :], q_wide[1, own, :]], axis=1).astype(BF16)
        scores = jnp.dot(q, keys_t[r], preferred_element_type=F32) * SCALE_INV
        position = d * POS + lax.broadcasted_iota(jnp.int32, (H, POS), 1)
        valid = position < lengths[r]
        masked = jnp.where(valid, scores, NEG)
        top = jnp.max(masked, axis=1, keepdims=True)
        weights = jnp.where(valid, jnp.exp(masked - top), 0.0)
        mass = jnp.sum(weights, axis=1, keepdims=True)
        summed = jnp.dot(weights.astype(BF16), values[r], preferred_element_type=F32)
        some = mass > 0.0
        safe = jnp.where(some, mass, 1.0)
        mean = summed / safe
        log_mass = jnp.where(some, top + jnp.log(safe), NEG)
        o_wide[0, own, :] = mean[:, :LANES]
        o_wide[1, own, :] = mean[:, LANES:]
        o_wide[2, own, :] = jnp.broadcast_to(log_mass, (H, LANES))
        return carry

    lax.fori_loop(0, ROWS, attend, 0, unroll=UNROLL)

    pair_shape = (2 * ROWS, LANES)
    diagonal_pair = lane_of(pair_shape) == lax.broadcasted_iota(jnp.int32, pair_shape, 0)

    def pack(n, carry):
        j = peer(lax.rem(n, 16), 1 - lax.div(n, 16))
        rows = pl.ds(pl.multiple_of(j * 2 * ROWS, 2 * ROWS), 2 * ROWS)
        s4[j, :, :LANES] = o_wide[0, rows, :].astype(BF16)
        s4[j, :, LANES:] = o_wide[1, rows, :].astype(BF16)
        log_mass = o_wide[2, rows, :]
        s4_mass[j] = jnp.sum(jnp.where(diagonal_pair, log_mass, 0.0), axis=0, keepdims=True)

        @pl.when(n < N_DEV - 1)
        def _():
            send(3, s4.at[j], r4.at[d], p, j)
            send(12, s4_mass.at[j], r4_mass.at[d], p, j)

        return carry

    lax.fori_loop(0, N_DEV, pack, 0)
    r4[d] = s4[d]
    r4_mass[d] = s4_mass[d]

    @pl.when(adds_new)
    def _():
        landed(recv_sem, 13, r3_new, N_LINE - 1)

    @pl.when(jnp.logical_not(adds_new))
    def _():
        landed(recv_sem, 13, r3_new, N_LINE)

    def wide_new(first):
        pieces = [r3_new[owner].astype(F32) for owner in (first, first + 1)]
        new = [(piece[:ROWS] + piece[ROWS:]) * row_scale for piece in pieces]
        new = jnp.concatenate(new, axis=1).astype(BF16).astype(F32)
        return jnp.concatenate([new, new], axis=0)

    key_new = wide_new(0)
    value_new = wide_new(2)
    score_new = jnp.sum(query_rows.astype(F32) * key_new, axis=1, keepdims=True) * SCALE_INV

    landed(recv_sem, 3, r4, N_DEV - 1)

    landed(recv_sem, 12, r4_mass, N_DEV - 1)
    masses = jnp.broadcast_to(r4_mass[...], (N_DEV, *pair_shape))
    log_all = jnp.sum(jnp.where(diagonal_pair[None], masses, 0.0), axis=2, keepdims=True)
    top_all = jnp.maximum(jnp.max(log_all, axis=0), score_new)
    share = jnp.exp(log_all - top_all[None])
    fresh = jnp.exp(score_new - top_all)
    mass_all = jnp.sum(share, axis=0) + fresh
    numerator = jnp.sum(share * r4[...].astype(F32), axis=0)
    numerator = numerator + fresh.astype(BF16).astype(F32) * value_new
    attended = numerator / mass_all
    own_heads = jnp.concatenate([attended[:ROWS], attended[ROWS:]], axis=1).astype(BF16)

    f_out.wait()

    def group_at(i):
        return lax.rem(x + entry(FAR_GROUP_X, i), 4) * 2 + lax.rem(lax.div(y, 2) + entry(FAR_GROUP_Y, i), 2)

    def columns_of(g):
        return pl.ds(pl.multiple_of(g * GROUP_COLS, LANES), GROUP_COLS)

    def chunks_of(block):
        return tiles_to_chunks([block[:, t * LANES : (t + 1) * LANES] for t in range(GROUP_COLS // LANES)])

    def project(i, carry):
        g = group_at(i)
        block = jnp.dot(own_heads, w_out[:, columns_of(g)], preferred_element_type=F32)
        for c, halves in enumerate(chunks_of(block)):
            j = g * GROUP + c
            s5[j] = jnp.concatenate(halves, axis=0).astype(BF16)

            @pl.when(j != d)
            def _():
                send(4, s5.at[j], r5.at[d], p, j)

        return carry

    lax.fori_loop(0, N_GROUP, project, 0)
    r5[d] = s5[d]

    turn = lax.rem(d * (COLS % LANES), LANES)
    back = lax.rem(LANES - turn, LANES)
    f_post_gain.wait()
    pad_gain[:, :COLS] = post_gain_v[...]
    lane = lane_of((ROWS, LANES))

    def unrotated(total):
        low_half = pltpu.roll(total[:ROWS], back, 1)
        high_half = pltpu.roll(total[ROWS:], back, 1)
        return low_half, jnp.where(lane < COLS - LANES, high_half, 0.0)

    landed(recv_sem, 4, r5, N_DEV - 1)
    attn_low, attn_high = unrotated(jnp.sum(r5[...].astype(F32), axis=0))
    res_low = pad_hidden[:, :LANES] + attn_low
    res_high = pad_hidden[:, LANES:] + attn_high
    row_squares = jnp.sum(res_low * res_low + res_high * res_high, axis=1, keepdims=True)
    coarse = row_squares.astype(BF16).astype(F32)
    fine = row_squares - coarse
    gained_low = res_low * pad_gain[:, :LANES]
    gained_high = res_high * pad_gain[:, LANES:]
    gained_high = jnp.where(lane == 96, coarse, jnp.where(lane == 97, fine, gained_high))
    tile = jnp.concatenate([pltpu.roll(gained_low, turn, 1), pltpu.roll(gained_high, turn, 1)], axis=0).astype(BF16)
    s6[...] = tile
    own = d * 2 + z_low
    r6[own] = tile

    def send_rows(n, carry):
        send(5, s6, r6.at[own], *peer_all(n))
        return carry

    lax.fori_loop(0, N_HALF - 1, send_rows, 0, unroll=21)
    landed(recv_sem, 5, r6, N_HALF - 1)

    some_rows = 2 * ROWS

    def assemble(g, sums):
        first = pl.multiple_of(g * 2 * GROUP, 2 * GROUP)
        block = r6[pl.ds(first, 2 * GROUP)].astype(F32).reshape(GROUP, 2, 2, ROWS, LANES)
        chunks = [
            (block[c, :, 0].reshape(some_rows, LANES), block[c, :, 1].reshape(some_rows, LANES))
            for c in range(GROUP)
        ]
        x_all[:, columns_of(g)] = jnp.concatenate(chunks_to_tiles(chunks), axis=1).astype(BF16)
        return tuple(total + chunk[1] for total, chunk in zip(sums, chunks))

    zeros = jnp.zeros((some_rows, LANES), F32)
    sums = lax.fori_loop(0, N_GROUP, assemble, (zeros,) * GROUP)
    lane_all = lane_of((some_rows, LANES))
    squares_at = zeros
    for c in range(GROUP):
        at = (96 + c * (COLS % LANES)) % LANES
        squares_at = squares_at + jnp.where((lane_all == at) | (lane_all == at + 1), sums[c], 0.0)
    all_squares = jnp.sum(squares_at, axis=1, keepdims=True)
    norm = lax.rsqrt(all_squares * (1.0 / D) + EPS)

    f_gate.wait()
    f_up.wait()
    shared[0].wait_recv()
    shared[1].wait_recv()
    transposed = (((1,), (1,)), ((), ()))

    def hidden_units(weights):
        units = weights[...].reshape(2 * weights.shape[1], D)
        return lax.dot_general(units, x_all[...], transposed, preferred_element_type=F32).T * norm

    gate = hidden_units(w_gate)
    up = hidden_units(w_up)
    activated = (gate / (1.0 + jnp.exp(-gate)) * up).astype(BF16)

    f_down.wait()
    shared[2].wait_recv()

    def pass_on(i, carry):
        g = group_at(i)
        columns = columns_of(g)
        weights = w_down[:, :, columns].reshape(2 * w_down.shape[1], GROUP_COLS)
        block = jnp.dot(activated, weights, preferred_element_type=F32)
        for c, (low_half, high_half) in enumerate(chunks_of(block)):
            for q in range(2):
                rows = slice(q * ROWS, (q + 1) * ROWS)
                at = (g * GROUP + c) * 2 + q
                s7[at] = jnp.concatenate([low_half[rows], high_half[rows]], axis=0).astype(BF16)

                @pl.when(at != own)
                def _():
                    send(9, s7.at[at], r7.at[own], q * 2 + core, g * GROUP + c)

        return carry

    lax.fori_loop(0, N_GROUP, pass_on, 0)
    r7[own] = s7[own]

    @pl.when(gives_squares)
    def _():
        landed(send_sem, 11, sent_rows, N_DEV - 1)

    landed(send_sem, 0, r1, N_LINE - 1)
    landed(send_sem, 1, r2, N_DEV - 1)

    @pl.when(adds_new)
    def _():
        landed(send_sem, 13, r5, N_DEV - 1)

    @pl.when(jnp.logical_not(adds_new))
    def _():
        landed(send_sem, 10, r2_new, 1)

    landed(send_sem, 2, r3, N_DEV - 1)
    landed(send_sem, 3, r4, N_DEV - 1)
    landed(send_sem, 4, r5, N_DEV - 1)
    landed(send_sem, 5, r6, N_HALF - 1)
    for copy in shared:
        copy.wait_send()
    landed(send_sem, 12, r4_mass, N_DEV - 1)

    landed(recv_sem, 9, r7, N_HALF - 1)
    ffn_low, ffn_high = unrotated(jnp.sum(r7[...].astype(F32), axis=0))
    out_ref[:, :LANES] = res_low + ffn_low
    out_ref[:, LANES:] = (res_high + ffn_high)[:, : COLS - LANES]

    landed(send_sem, 9, r7, N_HALF - 1)


def local(
    hidden_in, in_gain, w_latent, q_gain, w_query, cache_keys, cache_values, lengths, w_out, post_gain,
    w_gate, w_up, w_down,
):
    operands = (
        hidden_in, in_gain[None, :], w_latent, q_gain[None, :], w_query, cache_keys, cache_values, lengths,
        w_out, post_gain[None, :], w_gate.T, w_up.T, w_down,
    )
    tile = (2 * ROWS, LANES)

    def like(array):
        return pltpu.VMEM(array.shape, array.dtype)

    scratch = [
        like(hidden_in),
        pltpu.VMEM((1, COLS), F32),
        pltpu.VMEM((1, QR), F32),
        pltpu.VMEM((1, COLS), F32),
        pltpu.SMEM(lengths.shape, jnp.int32),
        like(w_latent),
        like(w_query),
        like(cache_keys),
        like(cache_values),
        like(w_out),
        pltpu.VMEM((2, *w_gate.shape[::-1]), BF16),
        pltpu.VMEM((2, *w_up.shape[::-1]), BF16),
        pltpu.VMEM((2, *w_down.shape), BF16),
        pltpu.VMEM((ROWS, 2 * LANES), F32),
        pltpu.VMEM((1, 2 * LANES), F32),
        pltpu.VMEM((N_LINE, 6 * ROWS, LANES), BF16),
        pltpu.VMEM((N_LINE, 6 * ROWS, LANES), BF16),
        pltpu.VMEM((4 * ROWS, LANES), BF16),
        pltpu.VMEM((N_DEV, 4 * ROWS, LANES), BF16),
        pltpu.VMEM(tile, BF16),
        pltpu.VMEM((8, *tile), BF16),
        pltpu.VMEM(tile, BF16),
        pltpu.VMEM((N_LINE, *tile), BF16),
        pltpu.VMEM((1, LANES), F32),
        pltpu.VMEM((8, 1, LANES), F32),
        pltpu.VMEM((N_DEV, 1, LANES), F32),
        pltpu.VMEM((2 * ROWS, HD), BF16),
        pltpu.VMEM((N_DEV, 2 * ROWS, HD), BF16),
        pltpu.VMEM((HD // LANES, H * ROWS, LANES), F32),
        pltpu.VMEM((MSG // LANES, H * ROWS, LANES), F32),
        pltpu.VMEM((N_DEV, 2 * ROWS, HD), BF16),
        pltpu.VMEM((N_DEV, 2 * ROWS, HD), BF16),
        pltpu.VMEM((N_DEV, 1, LANES), F32),
        pltpu.VMEM((N_DEV, 1, LANES), F32),
        pltpu.VMEM((N_DEV, *tile), BF16),
        pltpu.VMEM((N_DEV, *tile), BF16),
        pltpu.VMEM(tile, BF16),
        pltpu.VMEM((N_HALF, *tile), BF16),
        pltpu.VMEM((2 * ROWS, D), BF16),
        pltpu.VMEM((N_HALF, *tile), BF16),
        pltpu.VMEM((N_HALF, *tile), BF16),
        pltpu.VMEM((ROWS, HD, POS), BF16),
        pltpu.SemaphoreType.DMA((14,)),
        pltpu.SemaphoreType.DMA((14,)),
        pltpu.SemaphoreType.DMA((14,)),
        pltpu.SemaphoreType.REGULAR((2,)),
    ]
    return pl.pallas_call(
        kernel,
        out_shape=pltpu.VMEM(hidden_in.shape, F32),
        in_specs=[pl.BlockSpec(memory_space=pl.ANY)] * len(operands),
        out_specs=pl.BlockSpec(memory_space=pltpu.VMEM),
        scratch_shapes=scratch,
        compiler_params=pltpu.CompilerParams(
            collective_id=0, has_side_effects=True, vmem_limit_bytes=56 * 2**20
        ),
    )(*operands)


def solution(mesh):
    placed = (
        P("pool", "dev"),
        P("dev"),
        P("dev", None),
        P(),
        P(None, "dev"),
        P("pool", "dev", None),
        P("pool", "dev", None),
        P("pool"),
        P("dev", None),
        P("dev"),
        P(None, ("pool", "dev")),
        P(None, ("pool", "dev")),
        P(("pool", "dev"), None),
    )
    return jax.shard_map(
        local, mesh=mesh, in_specs=placed, out_specs=P("pool", "dev"), check_vma=False
    )
```
